32 devices in a mesh: slab: 2 (over x), tm: 16 (over z, y, core), band: 1.
Axes of the slice: x: 2, y: 2, z: 4, core: 2. Of those that a mesh axis runs over, the one named last changes fastest.
Arguments:
- tokens: bfloat16 [64, 4, 128, 1024], P(('slab', 'tm'), 'band'), parts along dimension 0
- norm_gain: float32 [1024], replicated, may hold values from 0.1 to 1.9
- query_weight: bfloat16 [1024, 1024], replicated
- key_weight: bfloat16 [1024, 1024], replicated
- value_weight: bfloat16 [1024, 1024], replicated, may hold values from -0.1875 to 0.1875
- out_weight: bfloat16 [1024, 1024], replicated, may hold values from -3 to 3
- key_frames: int32 [4], P('slab'), parts along dimension 0, may hold values from 0 to 31, as said below
Outputs:
- updated: bfloat16 [64, 4, 128, 1024], P(('slab', 'tm'), 'band'), parts along dimension 0
The draws below stay inside these ranges and needn't reach their ends.
There are 2 independent parts, one for each index of `slab`. The reference program is written for one: setup_inputs(seed, part) draws one part's arguments, and reference() takes and returns one part's arrays. A program takes and returns all parts, laid end to end along the dimension named above; an argument that names none is the same for every part. Nothing has to cross between parts.
Inputs may be any that keep to these rules, and one draw needn't show every extreme that they name: key_frames[k] is 16 * k plus an offset of 0 to 15; the first keyframe is frame 0 and the last is frame 32 - 1.
All inputs are finite; a program needn't handle non-finite values.
Results may differ from the reference program's by a relative error of at most 0.0061.
Values may be sent and summed in bfloat16 or wider, within the bound.
A program may use at most 192 MiB of HBM per device.

```python
import jax
import jax.numpy as jnp
from jax import lax

D = 1024
HEAD_DIM = 64
BAND_TOK = 128
BANDS = 4
KEY_EVERY = 16
FRAME_REACH = 2
BAND_REACH = 1
FRAMES = 32
KEYS = 2


def shared_projection(key):
    base = jax.random.normal(jax.random.fold_in(key, 11), (D, D), jnp.float32) * D ** (-0.5)
    return base


def draw_tokens(key, part):
    key = jax.random.fold_in(key, 1)
    shape = (FRAMES, BANDS, BAND_TOK, D)
    normal_part = jnp.clip(jax.random.normal(jax.random.fold_in(key, 2), shape, jnp.float32), -6.0, 6.0)
    return normal_part.astype(jnp.bfloat16)


def draw_query_weight(key, part):
    base = shared_projection(key)
    return base.astype(jnp.bfloat16)


def draw_key_weight(key, part):
    key = jax.random.fold_in(key, 31)
    own = jax.random.normal(key, (D, D), jnp.float32) * D ** (-0.5)
    return own.astype(jnp.bfloat16)


def draw_key_frames(key, part):
    key = jax.random.fold_in(key, 41)
    offsets = jax.random.randint(key, (KEYS,), 0, KEY_EVERY, jnp.int32)
    offsets = offsets.at[KEYS - 1].set(KEY_EVERY - 1)
    offsets = offsets.at[0].set(0)
    return (KEY_EVERY * jnp.arange(KEYS, dtype=jnp.int32) + offsets).astype(jnp.int32)


def bell_draw(stream_key, dims, width, limit, kind=jnp.bfloat16):
    values = jax.random.normal(stream_key, dims, jnp.float32) * width
    return jnp.minimum(jnp.maximum(values, -limit), limit).astype(kind)


def setup_inputs(seed: int = 0, part: int = 0) -> dict:
    arg_keys = jax.random.split(jax.random.key(seed), 8)
    own_keys = jax.random.split(jax.random.fold_in(arg_keys[7], part), 8)
    return {
        "tokens": draw_tokens(jax.random.fold_in(jax.random.fold_in(arg_keys[7], part), 71), part),
        "norm_gain": jnp.clip(1.0 + 0.18 * jax.random.normal(arg_keys[1], (D,), jnp.float32), 0.1, 1.9),
        "query_weight": draw_query_weight(jax.random.fold_in(arg_keys[7], 71), part),
        "key_weight": draw_key_weight(jax.random.fold_in(arg_keys[7], 71), part),
        "value_weight": bell_draw(arg_keys[4], (D, D), D ** -0.5, 0.1875),
        "out_weight": bell_draw(arg_keys[5], (D, D), 4 ** -0.5, 3.0),
        "key_frames": draw_key_frames(jax.random.fold_in(jax.random.fold_in(arg_keys[7], part), 71), part),
    }


def widen(array_in):
    return lax.optimization_barrier(array_in).astype(jnp.float32)

def layer_norm(token_rows, norm_gain):
    rows_float = token_rows.astype(jnp.float32)
    centred = rows_float - lax.optimization_barrier(jnp.mean(rows_float, axis=-1, keepdims=True))
    variance = lax.optimization_barrier(jnp.mean(centred * centred, axis=-1, keepdims=True))
    return (centred * lax.rsqrt(variance + 1e-05) * norm_gain).astype(jnp.bfloat16)

def attend(queries, key_values, allowed, width_model):
    head_count = width_model // HEAD_DIM
    query_heads = widen(queries).reshape(queries.shape[0], head_count, HEAD_DIM)
    key_heads = widen(key_values[:, :width_model]).reshape(-1, head_count, HEAD_DIM)
    value_heads = widen(key_values[:, width_model:]).reshape(-1, head_count, HEAD_DIM)
    scores = jnp.einsum('qhd,khd->hqk', query_heads, key_heads) * HEAD_DIM ** (-0.5)
    scores = jnp.where(allowed[None], scores, jnp.float32(-1e+30))
    largest = lax.optimization_barrier(jnp.max(scores, axis=-1, keepdims=True))
    weights = jnp.exp(scores - largest)
    denominator = lax.optimization_barrier(jnp.sum(weights, axis=-1))
    probs = widen(weights.astype(jnp.bfloat16))
    context = jnp.einsum('hqk,khd->qhd', probs, value_heads) / jnp.transpose(denominator)[:, :, None]
    return context.reshape(queries.shape[0], width_model).astype(jnp.bfloat16)

def reference(tokens, norm_gain, query_weight, key_weight, value_weight, out_weight, key_frames):
    frame_count, band_count, band_tokens, width_model = tokens.shape
    token_rows = tokens.reshape(-1, width_model)
    normed = layer_norm(token_rows, norm_gain)
    queries = jnp.dot(normed, query_weight, preferred_element_type=jnp.float32).astype(jnp.bfloat16)
    key_rows = jnp.dot(normed, key_weight, preferred_element_type=jnp.float32).astype(jnp.bfloat16)
    values = jnp.dot(normed, value_weight, preferred_element_type=jnp.float32).astype(jnp.bfloat16)
    queries = queries.reshape(frame_count, band_count * band_tokens, width_model)
    key_value = jnp.concatenate([key_rows, values], axis=1).reshape(frame_count, band_count, band_tokens, 2 * width_model)
    padded = jnp.pad(key_value, ((FRAME_REACH, FRAME_REACH), (0, 0), (0, 0), (0, 0)))
    keyframe_rows = key_value[key_frames.astype(jnp.int32)].reshape(-1, 2 * width_model)
    span = 2 * FRAME_REACH + 1
    query_band = jnp.broadcast_to(jnp.arange(band_count, dtype=jnp.int32)[:, None], (band_count, band_tokens)).reshape(-1)
    window_band = jnp.broadcast_to(jnp.arange(band_count, dtype=jnp.int32)[None, :, None], (span, band_count, band_tokens)).reshape(-1)
    keyframe_band = jnp.broadcast_to(jnp.arange(band_count, dtype=jnp.int32)[None, :, None], (key_frames.shape[0], band_count, band_tokens)).reshape(-1)
    keyframe_frame = jnp.broadcast_to(key_frames.astype(jnp.int32)[:, None, None], (key_frames.shape[0], band_count, band_tokens)).reshape(-1)

    def one_frame(frame):
        window = lax.dynamic_slice_in_dim(padded, frame, span, 0).reshape(-1, 2 * width_model)
        window_frame = jnp.broadcast_to((frame - FRAME_REACH + jnp.arange(span, dtype=jnp.int32))[:, None, None], (span, band_count, band_tokens)).reshape(-1)
        allowed_window = (window_frame[None, :] >= 0) & (window_frame[None, :] < frame_count) & (jnp.abs(query_band[:, None] - window_band[None, :]) <= BAND_REACH)
        allowed_keyframe = (query_band[:, None] == keyframe_band[None, :]) & (jnp.abs(frame - keyframe_frame[None, :]) > FRAME_REACH)
        allowed = jnp.concatenate([allowed_window, allowed_keyframe], axis=1)
        key_values = jnp.concatenate([window, keyframe_rows], axis=0)
        frame_queries = lax.dynamic_index_in_dim(queries, frame, 0, keepdims=False)
        return attend(frame_queries, key_values, allowed, width_model)
    context = lax.map(one_frame, jnp.arange(frame_count, dtype=jnp.int32)).reshape(-1, width_model)
    updated = token_rows.astype(jnp.float32) + jnp.dot(context, out_weight, preferred_element_type=jnp.float32)
    return updated.astype(jnp.bfloat16).reshape(frame_count, band_count, band_tokens, width_model)
```

```python
import functools
import math

import jax
import jax.numpy as jnp
from jax import lax
from jax.experimental import pallas as pl
from jax.experimental.pallas import tpu as pltpu
from jax.sharding import PartitionSpec as P

HEAD_DIM = 64
FRAME_REACH = 2
BAND_REACH = 1


def padded(cells, sides, width):
    for axis, dim in sides:
        count = lax.axis_size(axis)
        ends = count - 1
        head = lax.slice_in_dim(cells, 0, width, axis=dim)
        tail = lax.slice_in_dim(cells, cells.shape[dim] - width, cells.shape[dim], axis=dim)
        cells = jnp.concatenate(
            [
                lax.ppermute(tail, axis, [(i, (i + 1) % count) for i in range(ends)]),
                cells,
                lax.ppermute(head, axis, [((i + 1) % count, i) for i in range(ends)]),
            ],
            axis=dim,
        )
    return cells


def from_root(array, axis, root):
    mine = lax.axis_index(axis) == root
    return lax.psum(jnp.where(mine, array, jnp.zeros_like(array)), axis)


def layer_norm(token_rows, norm_gain):
    rows_float = token_rows.astype(jnp.float32)
    centred = rows_float - jnp.mean(rows_float, axis=-1, keepdims=True)
    variance = jnp.mean(centred * centred, axis=-1, keepdims=True)
    return (centred * lax.rsqrt(variance + 1e-05) * norm_gain).astype(jnp.bfloat16)


def attend(queries, key_values, allowed, width_model):
    head_count = width_model // HEAD_DIM
    query_heads = queries.reshape(queries.shape[0], head_count, HEAD_DIM)
    key_heads = key_values[:, :width_model].reshape(-1, head_count, HEAD_DIM)
    value_heads = key_values[:, width_model:].reshape(-1, head_count, HEAD_DIM)
    scores = jnp.einsum(
        "qhd,khd->hqk", query_heads, key_heads, preferred_element_type=jnp.float32
    ) * HEAD_DIM ** (-0.5)
    scores = jnp.where(allowed[None, None, :], scores, jnp.float32(-1e30))
    largest = jnp.max(scores, axis=-1, keepdims=True)
    weights = jnp.exp(scores - largest)
    denominator = jnp.sum(weights, axis=-1)
    probs = weights.astype(jnp.bfloat16)
    context = jnp.einsum("hqk,khd->qhd", probs, value_heads, preferred_element_type=jnp.float32)
    context = context / jnp.transpose(denominator)[:, :, None]
    return context.reshape(queries.shape[0], width_model).astype(jnp.bfloat16)


def per_device(tokens, norm_gain, query_weight, key_weight, value_weight, out_weight, key_frames):
    frame_count, band_count, band_tokens, width_model = tokens.shape
    token_rows = tokens.reshape(-1, width_model)
    normed = layer_norm(token_rows, norm_gain)
    queries = jnp.dot(normed, query_weight, preferred_element_type=jnp.float32).astype(jnp.bfloat16)
    key_rows = jnp.dot(normed, key_weight, preferred_element_type=jnp.float32).astype(jnp.bfloat16)
    values = jnp.dot(normed, value_weight, preferred_element_type=jnp.float32).astype(jnp.bfloat16)
    queries = queries.reshape(frame_count, band_count, band_tokens, width_model)
    key_value = jnp.concatenate([key_rows, values], axis=1).reshape(
        frame_count, band_count, band_tokens, 2 * width_model
    )
    banded = padded(key_value, (("band", 1),), BAND_REACH)
    extended = padded(banded, (("tm", 0),), FRAME_REACH)
    first_frame = lax.axis_index("tm") * frame_count
    first_band = lax.axis_index("band") * band_count
    frames_total = lax.axis_size("tm") * frame_count
    bands_total = lax.axis_size("band") * band_count
    keyframe_count = key_frames.shape[0]

    def fetch(number, store):
        target = key_frames[number]
        owner = target // frame_count
        local = jnp.clip(target - first_frame, 0, frame_count - 1)
        candidate = lax.dynamic_index_in_dim(key_value, local, 0, keepdims=False)
        arrived = from_root(candidate, "tm", owner)
        return lax.dynamic_update_index_in_dim(store, arrived, number, 0)

    empty = jnp.zeros((keyframe_count, band_count, band_tokens, 2 * width_model), jnp.bfloat16)
    keyframe_store = lax.fori_loop(0, keyframe_count, fetch, empty)
    frame_span = 2 * FRAME_REACH + 1
    band_span = 2 * BAND_REACH + 1

    def one_block(number):
        frame_local = number // band_count
        band_local = number % band_count
        window = lax.dynamic_slice(
            extended,
            (frame_local, band_local, 0, 0),
            (frame_span, band_span, band_tokens, 2 * width_model),
        )
        frame_now = first_frame + frame_local
        band_now = first_band + band_local
        window_frame = frame_now - FRAME_REACH + jnp.arange(frame_span, dtype=jnp.int32)
        window_band = band_now - BAND_REACH + jnp.arange(band_span, dtype=jnp.int32)
        frame_valid = (window_frame >= 0) & (window_frame < frames_total)
        band_valid = (window_band >= 0) & (window_band < bands_total)
        allowed_window = jnp.broadcast_to(
            (frame_valid[:, None] & band_valid[None, :])[:, :, None],
            (frame_span, band_span, band_tokens),
        ).reshape(-1)
        allowed_keyframe = jnp.broadcast_to(
            (jnp.abs(frame_now - key_frames) > FRAME_REACH)[:, None], (keyframe_count, band_tokens)
        ).reshape(-1)
        allowed = jnp.concatenate([allowed_window, allowed_keyframe], axis=0)
        keyframe_band = lax.dynamic_index_in_dim(keyframe_store, band_local, 1, keepdims=False)
        key_values = jnp.concatenate(
            [window.reshape(-1, 2 * width_model), keyframe_band.reshape(-1, 2 * width_model)],
            axis=0,
        )
        block_queries = lax.dynamic_index_in_dim(
            lax.dynamic_index_in_dim(queries, frame_local, 0, keepdims=False),
            band_local,
            0,
            keepdims=False,
        )
        return attend(block_queries, key_values, allowed, width_model)

    context = lax.map(one_block, jnp.arange(frame_count * band_count, dtype=jnp.int32)).reshape(
        -1, width_model
    )
    updated = token_rows.astype(jnp.float32) + jnp.dot(
        context, out_weight, preferred_element_type=jnp.float32
    )
    return updated.astype(jnp.bfloat16).reshape(frame_count, band_count, band_tokens, width_model)


LANES = 128
NEG = -1e30


def fused_kernel(
    frames, bands, band_tokens, keys,
    valid_ref, left_ref, own_ref, right_ref, key_ref, gain_ref,
    wq_ref, wk_ref, wv_ref, wo_ref, out_ref,
    normed, kbuf, vbuf, qbuf, context,
):
    step = pl.program_id(0)
    group = wq_ref.shape[1]
    frame_rows = bands * band_tokens
    reach_rows = FRAME_REACH * frame_rows
    own_rows = frames * frame_rows
    ext_rows = normed.shape[0]
    sources = (
        (left_ref, 0, reach_rows),
        (own_ref, reach_rows, own_rows),
        (right_ref, reach_rows + own_rows, reach_rows),
        (key_ref, 2 * reach_rows + own_rows, keys * frame_rows),
    )

    @pl.when(step == 0)
    def _():
        for source, base, count in sources:

            @pl.loop(0, count // LANES)
            def _(i):
                rows = source[pl.ds(pl.multiple_of(i * LANES, LANES), LANES), :].astype(jnp.float32)
                centred = rows - jnp.mean(rows, axis=-1, keepdims=True)
                variance = jnp.mean(centred * centred, axis=-1, keepdims=True)
                normed[pl.ds(pl.multiple_of(base + i * LANES, LANES), LANES), :] = (
                    centred * lax.rsqrt(variance + 1e-05) * gain_ref[...]
                ).astype(jnp.bfloat16)

    chunk = 512

    @pl.loop(0, ext_rows // chunk)
    def _(i):
        at = pl.ds(pl.multiple_of(i * chunk, chunk), chunk)
        rows = normed[at, :]
        kbuf[at, :] = jnp.dot(rows, wk_ref[...], preferred_element_type=jnp.float32).astype(jnp.bfloat16)
        vbuf[at, :] = jnp.dot(rows, wv_ref[...], preferred_element_type=jnp.float32).astype(jnp.bfloat16)

    @pl.loop(0, own_rows // chunk)
    def _(i):
        rows = normed[pl.ds(pl.multiple_of(reach_rows + i * chunk, chunk), chunk), :]
        q = jnp.dot(rows, wq_ref[...], preferred_element_type=jnp.float32)
        qbuf[pl.ds(pl.multiple_of(i * chunk, chunk), chunk), :] = (
            q * (HEAD_DIM ** (-0.5) * math.log2(math.e))
        ).astype(jnp.bfloat16)

    span = 2 * FRAME_REACH + 1
    low = lax.broadcasted_iota(jnp.int32, (band_tokens, LANES), 1) < HEAD_DIM

    @pl.loop(0, frames * (group // LANES))
    def _(number):
        frame = number // (group // LANES)
        pair = number % (group // LANES)
        lanes = pl.ds(pl.multiple_of(pair * LANES, LANES), LANES)
        for band in range(bands):
            first = max(band - BAND_REACH, 0)
            count = min(band + BAND_REACH, bands - 1) + 1 - first
            at_q = pl.ds(pl.multiple_of(frame * frame_rows + band * band_tokens, band_tokens), band_tokens)
            q = qbuf[at_q, lanes]
            zero = jnp.zeros_like(q)
            q2 = jnp.concatenate([jnp.where(low, q, zero), jnp.where(low, zero, q)], axis=0)
            places = [
                pl.ds(
                    pl.multiple_of((frame + j) * frame_rows + first * band_tokens, band_tokens),
                    count * band_tokens,
                )
                for j in range(span)
            ] + [
                pl.ds(2 * reach_rows + own_rows + k * frame_rows + band * band_tokens, band_tokens)
                for k in range(keys)
            ]
            scores = []
            for j, place in enumerate(places):
                s = lax.dot_general(
                    q2, kbuf[place, lanes], (((1,), (1,)), ((), ())),
                    preferred_element_type=jnp.float32,
                )
                if j != FRAME_REACH:
                    s = jnp.where(valid_ref[frame, j] > 0, s, NEG)
                scores.append(s)
            largest = functools.reduce(
                jnp.maximum, [jnp.max(s, axis=-1, keepdims=True) for s in scores]
            )
            total = jnp.zeros((2 * band_tokens, LANES), jnp.float32)
            denominator = jnp.zeros((2 * band_tokens, 1), jnp.float32)
            for s, place in zip(scores, places):
                weights = jnp.exp2(s - largest)
                denominator += jnp.sum(weights, axis=-1, keepdims=True)
                total += jnp.dot(
                    weights.astype(jnp.bfloat16), vbuf[place, lanes],
                    preferred_element_type=jnp.float32,
                )
            total = total / denominator
            block = jnp.where(low, total[:band_tokens], total[band_tokens:])
            context[at_q, pl.ds(pl.multiple_of(step * group + pair * LANES, LANES), LANES)] = block.astype(
                jnp.bfloat16
            )

    @pl.when(step == pl.num_programs(0) - 1)
    def _():
        @pl.loop(0, own_rows // 256)
        def _(i):
            at = pl.ds(pl.multiple_of(i * 256, 256), 256)
            out_ref[at, :] = (
                own_ref[at, :].astype(jnp.float32)
                + jnp.dot(context[at, :], wo_ref[...], preferred_element_type=jnp.float32)
            ).astype(jnp.bfloat16)


def fused(tokens, norm_gain, query_weight, key_weight, value_weight, out_weight, key_frames):
    frame_count, band_count, band_tokens, width_model = tokens.shape
    frame_rows = band_count * band_tokens
    keyframe_count = key_frames.shape[0]
    size = lax.axis_size("tm")
    me = lax.axis_index("tm")
    frames_total = size * frame_count
    left = lax.ppermute(
        tokens[frame_count - FRAME_REACH:], "tm", [(i, i + 1) for i in range(size - 1)]
    )
    right = lax.ppermute(tokens[:FRAME_REACH], "tm", [(i + 1, i) for i in range(size - 1)])
    first_frame = me * frame_count
    parts = []
    for number in range(keyframe_count):
        target = key_frames[number]
        local = target - first_frame
        mine = (local >= 0) & (local < frame_count)
        part = lax.dynamic_index_in_dim(tokens, jnp.clip(local, 0, frame_count - 1), 0, keepdims=True)
        parts.append(jnp.where(mine, part, jnp.zeros_like(part)))
    key_tokens = lax.psum(jnp.concatenate(parts, axis=0), "tm")
    frame_now = first_frame + jnp.arange(frame_count, dtype=jnp.int32)
    window = frame_now[:, None] - FRAME_REACH + jnp.arange(2 * FRAME_REACH + 1, dtype=jnp.int32)[None]
    valid = jnp.concatenate(
        [
            (window >= 0) & (window < frames_total),
            jnp.abs(frame_now[:, None] - key_frames[None]) > FRAME_REACH,
        ],
        axis=1,
    )
    group = 256
    ext_rows = (2 * FRAME_REACH + frame_count + keyframe_count) * frame_rows
    own_rows = frame_count * frame_rows
    whole = lambda shape: pl.BlockSpec(shape, lambda i: (0, 0), pipeline_mode=pl.Buffered(1))
    columns = pl.BlockSpec((width_model, group), lambda i: (0, i))
    out = pl.pallas_call(
        functools.partial(fused_kernel, frame_count, band_count, band_tokens, keyframe_count),
        grid=(width_model // group,),
        out_shape=jax.ShapeDtypeStruct((own_rows, width_model), jnp.bfloat16),
        in_specs=[
            pl.BlockSpec(memory_space=pltpu.SMEM),
            whole((FRAME_REACH * frame_rows, width_model)),
            whole((own_rows, width_model)),
            whole((FRAME_REACH * frame_rows, width_model)),
            whole((keyframe_count * frame_rows, width_model)),
            whole((1, width_model)),
            columns, columns, columns,
            whole((width_model, width_model)),
        ],
        out_specs=whole((own_rows, width_model)),
        scratch_shapes=[
            pltpu.VMEM((ext_rows, width_model), jnp.bfloat16),
            pltpu.VMEM((ext_rows, group), jnp.bfloat16),
            pltpu.VMEM((ext_rows, group), jnp.bfloat16),
            pltpu.VMEM((own_rows, group), jnp.bfloat16),
            pltpu.VMEM((own_rows, width_model), jnp.bfloat16),
        ],
        compiler_params=pltpu.CompilerParams(vmem_limit_bytes=56 * 2 ** 20),
    )(
        valid.astype(jnp.int32),
        left.reshape(-1, width_model), tokens.reshape(-1, width_model), right.reshape(-1, width_model),
        key_tokens.reshape(-1, width_model), norm_gain.reshape(1, -1),
        query_weight, key_weight, value_weight, out_weight,
    )
    return out.reshape(tokens.shape)


def solution(mesh):
    body = fused if mesh.shape["band"] == 1 else per_device
    in_specs = (P(("slab", "tm"), "band", None, None), P(), P(), P(), P(), P(), P("slab"))
    out_specs = P(("slab", "tm"), "band", None, None)
    return jax.shard_map(
        body, mesh=mesh, in_specs=in_specs, out_specs=out_specs, check_vma=False
    )
```

```python
import functools
import math

import jax
import jax.numpy as jnp
from jax import lax
from jax.experimental import pallas as pl
from jax.experimental.pallas import tpu as pltpu
from jax.sharding import PartitionSpec as P

HEAD_DIM = 64
FRAME_REACH = 2
BAND_REACH = 1


def padded(cells, sides, width):
    for axis, dim in sides:
        count = lax.axis_size(axis)
        ends = count - 1
        head = lax.slice_in_dim(cells, 0, width, axis=dim)
        tail = lax.slice_in_dim(cells, cells.shape[dim] - width, cells.shape[dim], axis=dim)
        cells = jnp.concatenate(
            [
                lax.ppermute(tail, axis, [(i, (i + 1) % count) for i in range(ends)]),
                cells,
                lax.ppermute(head, axis, [((i + 1) % count, i) for i in range(ends)]),
            ],
            axis=dim,
        )
    return cells


def from_root(array, axis, root):
    mine = lax.axis_index(axis) == root
    return lax.psum(jnp.where(mine, array, jnp.zeros_like(array)), axis)


def layer_norm(token_rows, norm_gain):
    rows_float = token_rows.astype(jnp.float32)
    centred = rows_float - jnp.mean(rows_float, axis=-1, keepdims=True)
    variance = jnp.mean(centred * centred, axis=-1, keepdims=True)
    return (centred * lax.rsqrt(variance + 1e-05) * norm_gain).astype(jnp.bfloat16)


def attend(queries, key_values, allowed, width_model):
    head_count = width_model // HEAD_DIM
    query_heads = queries.reshape(queries.shape[0], head_count, HEAD_DIM)
    key_heads = key_values[:, :width_model].reshape(-1, head_count, HEAD_DIM)
    value_heads = key_values[:, width_model:].reshape(-1, head_count, HEAD_DIM)
    scores = jnp.einsum(
        "qhd,khd->hqk", query_heads, key_heads, preferred_element_type=jnp.float32
    ) * HEAD_DIM ** (-0.5)
    scores = jnp.where(allowed[None, None, :], scores, jnp.float32(-1e30))
    largest = jnp.max(scores, axis=-1, keepdims=True)
    weights = jnp.exp(scores - largest)
    denominator = jnp.sum(weights, axis=-1)
    probs = weights.astype(jnp.bfloat16)
    context = jnp.einsum("hqk,khd->qhd", probs, value_heads, preferred_element_type=jnp.float32)
    context = context / jnp.transpose(denominator)[:, :, None]
    return context.reshape(queries.shape[0], width_model).astype(jnp.bfloat16)


def per_device(tokens, norm_gain, query_weight, key_weight, value_weight, out_weight, key_frames):
    frame_count, band_count, band_tokens, width_model = tokens.shape
    token_rows = tokens.reshape(-1, width_model)
    normed = layer_norm(token_rows, norm_gain)
    queries = jnp.dot(normed, query_weight, preferred_element_type=jnp.float32).astype(jnp.bfloat16)
    key_rows = jnp.dot(normed, key_weight, preferred_element_type=jnp.float32).astype(jnp.bfloat16)
    values = jnp.dot(normed, value_weight, preferred_element_type=jnp.float32).astype(jnp.bfloat16)
    queries = queries.reshape(frame_count, band_count, band_tokens, width_model)
    key_value = jnp.concatenate([key_rows, values], axis=1).reshape(
        frame_count, band_count, band_tokens, 2 * width_model
    )
    banded = padded(key_value, (("band", 1),), BAND_REACH)
    extended = padded(banded, (("tm", 0),), FRAME_REACH)
    first_frame = lax.axis_index("tm") * frame_count
    first_band = lax.axis_index("band") * band_count
    frames_total = lax.axis_size("tm") * frame_count
    bands_total = lax.axis_size("band") * band_count
    keyframe_count = key_frames.shape[0]

    def fetch(number, store):
        target = key_frames[number]
        owner = target // frame_count
        local = jnp.clip(target - first_frame, 0, frame_count - 1)
        candidate = lax.dynamic_index_in_dim(key_value, local, 0, keepdims=False)
        arrived = from_root(candidate, "tm", owner)
        return lax.dynamic_update_index_in_dim(store, arrived, number, 0)

    empty = jnp.zeros((keyframe_count, band_count, band_tokens, 2 * width_model), jnp.bfloat16)
    keyframe_store = lax.fori_loop(0, keyframe_count, fetch, empty)
    frame_span = 2 * FRAME_REACH + 1
    band_span = 2 * BAND_REACH + 1

    def one_block(number):
        frame_local = number // band_count
        band_local = number % band_count
        window = lax.dynamic_slice(
            extended,
            (frame_local, band_local, 0, 0),
            (frame_span, band_span, band_tokens, 2 * width_model),
        )
        frame_now = first_frame + frame_local
        band_now = first_band + band_local
        window_frame = frame_now - FRAME_REACH + jnp.arange(frame_span, dtype=jnp.int32)
        window_band = band_now - BAND_REACH + jnp.arange(band_span, dtype=jnp.int32)
        frame_valid = (window_frame >= 0) & (window_frame < frames_total)
        band_valid = (window_band >= 0) & (window_band < bands_total)
        allowed_window = jnp.broadcast_to(
            (frame_valid[:, None] & band_valid[None, :])[:, :, None],
            (frame_span, band_span, band_tokens),
        ).reshape(-1)
        allowed_keyframe = jnp.broadcast_to(
            (jnp.abs(frame_now - key_frames) > FRAME_REACH)[:, None], (keyframe_count, band_tokens)
        ).reshape(-1)
        allowed = jnp.concatenate([allowed_window, allowed_keyframe], axis=0)
        keyframe_band = lax.dynamic_index_in_dim(keyframe_store, band_local, 1, keepdims=False)
        key_values = jnp.concatenate(
            [window.reshape(-1, 2 * width_model), keyframe_band.reshape(-1, 2 * width_model)],
            axis=0,
        )
        block_queries = lax.dynamic_index_in_dim(
            lax.dynamic_index_in_dim(queries, frame_local, 0, keepdims=False),
            band_local,
            0,
            keepdims=False,
        )
        return attend(block_queries, key_values, allowed, width_model)

    context = lax.map(one_block, jnp.arange(frame_count * band_count, dtype=jnp.int32)).reshape(
        -1, width_model
    )
    updated = token_rows.astype(jnp.float32) + jnp.dot(
        context, out_weight, preferred_element_type=jnp.float32
    )
    return updated.astype(jnp.bfloat16).reshape(frame_count, band_count, band_tokens, width_model)


LANES = 128
NEG = -1e30


def fused_kernel(
    frames, bands, band_tokens, keys,
    valid_ref, left_ref, own_ref, right_ref, key_ref, gain_ref,
    q_ref, k_ref, v_ref, wk_ref, wv_ref, wo_ref, out_ref,
    normed, kbuf, vbuf, context,
):
    step = pl.program_id(0)
    group = wk_ref.shape[1]
    frame_rows = bands * band_tokens
    reach_rows = FRAME_REACH * frame_rows
    own_rows = frames * frame_rows
    sources = (
        (left_ref, 0, reach_rows),
        (right_ref, reach_rows + own_rows, reach_rows),
        (key_ref, 2 * reach_rows + own_rows, keys * frame_rows),
    )

    @pl.when(step == 0)
    def _():
        for source, base, count in sources:

            @pl.loop(0, count // LANES)
            def _(i):
                rows = source[pl.ds(pl.multiple_of(i * LANES, LANES), LANES), :]
                normed[pl.ds(pl.multiple_of(base + i * LANES, LANES), LANES), :] = normalise(rows, gain_ref[...])

    chunk = 512
    for _, base, count in sources:

        @pl.loop(0, count // chunk)
        def _(i):
            at = pl.ds(pl.multiple_of(base + i * chunk, chunk), chunk)
            rows = normed[at, :]
            kbuf[at, :] = jnp.dot(rows, wk_ref[...], preferred_element_type=jnp.float32).astype(jnp.bfloat16)
            vbuf[at, :] = jnp.dot(rows, wv_ref[...], preferred_element_type=jnp.float32).astype(jnp.bfloat16)

    kbuf[pl.ds(reach_rows, own_rows), :] = k_ref[...]
    vbuf[pl.ds(reach_rows, own_rows), :] = v_ref[...]

    span = 2 * FRAME_REACH + 1
    low = lax.broadcasted_iota(jnp.int32, (band_tokens, LANES), 1) < HEAD_DIM

    @pl.loop(0, frames * (group // LANES))
    def _(number):
        frame = number // (group // LANES)
        pair = number % (group // LANES)
        lanes = pl.ds(pl.multiple_of(pair * LANES, LANES), LANES)
        for band in range(bands):
            first = max(band - BAND_REACH, 0)
            count = min(band + BAND_REACH, bands - 1) + 1 - first
            at_q = pl.ds(pl.multiple_of(frame * frame_rows + band * band_tokens, band_tokens), band_tokens)
            q = q_ref[at_q, lanes]
            zero = jnp.zeros_like(q)
            q2 = jnp.concatenate([jnp.where(low, q, zero), jnp.where(low, zero, q)], axis=0)
            places = [
                pl.ds(
                    pl.multiple_of((frame + j) * frame_rows + first * band_tokens, band_tokens),
                    count * band_tokens,
                )
                for j in range(span)
            ] + [
                pl.ds(2 * reach_rows + own_rows + k * frame_rows + band * band_tokens, band_tokens)
                for k in range(keys)
            ]
            scores = []
            for j, place in enumerate(places):
                s = lax.dot_general(
                    q2, kbuf[place, lanes], (((1,), (1,)), ((), ())),
                    preferred_element_type=jnp.float32,
                )
                if j != FRAME_REACH:
                    s = jnp.where(valid_ref[frame, j] > 0, s, NEG)
                scores.append(s)
            largest = functools.reduce(
                jnp.maximum, [jnp.max(s, axis=-1, keepdims=True) for s in scores]
            )
            total = jnp.zeros((2 * band_tokens, LANES), jnp.float32)
            denominator = jnp.zeros((2 * band_tokens, 1), jnp.float32)
            for s, place in zip(scores, places):
                weights = jnp.exp2(s - largest)
                denominator += jnp.sum(weights, axis=-1, keepdims=True)
                total += jnp.dot(
                    weights.astype(jnp.bfloat16), vbuf[place, lanes],
                    preferred_element_type=jnp.float32,
                )
            total = total / denominator
            block = jnp.where(low, total[:band_tokens], total[band_tokens:])
            context[at_q, pl.ds(pl.multiple_of(step * group + pair * LANES, LANES), LANES)] = block.astype(
                jnp.bfloat16
            )

    @pl.when(step == pl.num_programs(0) - 1)
    def _():
        @pl.loop(0, own_rows // 256)
        def _(i):
            at = pl.ds(pl.multiple_of(i * 256, 256), 256)
            out_ref[at, :] = (
                own_ref[at, :].astype(jnp.float32)
                + jnp.dot(context[at, :], wo_ref[...], preferred_element_type=jnp.float32)
            ).astype(jnp.bfloat16)


KEY_CHUNKS = 4


def normalise(rows, gain):
    rows = rows.astype(jnp.float32)
    centred = rows - jnp.mean(rows, axis=-1, keepdims=True)
    variance = jnp.mean(centred * centred, axis=-1, keepdims=True)
    return (centred * lax.rsqrt(variance + 1e-05) * gain).astype(jnp.bfloat16)


def exchange_kernel(
    size, frame_rows,
    tokens_ref, gain_ref, wq_hbm, wk_hbm, wv_hbm,
    left_ref, right_ref, key_ref, q_ref, k_ref, v_ref,
    own, wq, wk, wv, halo_send, halo_recv, key_send, key_recv, local_sem, edge_sem, root_sem,
):
    me = lax.axis_index("tm")
    place = lax.rem(me, 4)
    own_rows = tokens_ref.shape[0]
    reach_rows = FRAME_REACH * frame_rows
    across = jnp.where(place < 2, me + 2, me - 2)
    corner = (place == 0) | (place == 3)
    partners = (
        (me > 0, me - 1),
        (me < size - 1, me + 1),
        (me >= 0, across),
        (corner & (me >= 4), me - 4),
        (corner & (me < size - 4), me + 4),
    )
    barrier = pltpu.get_barrier_semaphore()
    expected = 0
    for there, device in partners:
        expected = expected + jnp.where(there, 1, 0)

        @pl.when(there)
        def _():
            pl.semaphore_signal(
                barrier, inc=1, device_id={"tm": device}, device_id_type=pl.DeviceIdType.MESH
            )

    pl.semaphore_wait(barrier, expected)

    part = frame_rows // KEY_CHUNKS

    def children(k):
        j = me if k == 0 else size - 1 - me
        sign = 1 if k == 0 else -1
        r = lax.rem(j, 4)
        return j, (
            ((r == 0) & (j < size - 4), me + 4 * sign),
            (r == 0, me + 2 * sign),
            (lax.rem(j, 2) == 0, me + sign),
        )

    def key_copy(k, c, child, device, source, base):
        return pltpu.make_async_remote_copy(
            src_ref=source.at[pl.ds(base + c * part, part), :],
            dst_ref=key_ref.at[pl.ds(k * frame_rows + c * part, part), :],
            send_sem=key_send.at[k, c, child],
            recv_sem=key_recv.at[k, c],
            device_id={"tm": device},
            device_id_type=pl.DeviceIdType.MESH,
        )

    for k in range(2):
        j, targets = children(k)
        base = 0 if k == 0 else own_rows - frame_rows

        @pl.when(j == 0)
        def _():
            for c in range(KEY_CHUNKS):
                for child, (there, device) in enumerate(targets):
                    key_copy(k, c, child, device, tokens_ref, base).start()
            pltpu.make_async_copy(
                tokens_ref.at[pl.ds(base, frame_rows), :],
                key_ref.at[pl.ds(k * frame_rows, frame_rows), :],
                root_sem.at[k],
            ).start()

    halos = []
    for side, (there, device, base, target) in enumerate((
        (me < size - 1, me + 1, own_rows - reach_rows, left_ref),
        (me > 0, me - 1, 0, right_ref),
    )):
        remote = pltpu.make_async_remote_copy(
            src_ref=tokens_ref.at[pl.ds(base, reach_rows), :],
            dst_ref=target,
            send_sem=halo_send.at[side],
            recv_sem=halo_recv.at[side],
            device_id={"tm": device},
            device_id_type=pl.DeviceIdType.MESH,
        )
        edge = pltpu.make_async_copy(
            tokens_ref.at[pl.ds(base, reach_rows), :], target, edge_sem.at[side]
        )
        receives = me > 0 if side == 0 else me < size - 1
        halos.append((there, receives, remote, edge))

        @pl.when(there)
        def _():
            remote.start()

        @pl.when(jnp.logical_not(receives))
        def _():
            edge.start()

    loads = [
        pltpu.make_async_copy(source, target, local_sem.at[i])
        for i, (source, target) in enumerate(
            ((tokens_ref, own), (wq_hbm, wq), (wk_hbm, wk), (wv_hbm, wv))
        )
    ]
    for load in loads:
        load.start()
    for load in loads:
        load.wait()

    step_rows = own_rows // KEY_CHUNKS
    for c in range(KEY_CHUNKS):
        for k in range(2):
            j, targets = children(k)

            @pl.when(j > 0)
            def _():
                key_copy(k, c, 0, across, key_ref, k * frame_rows).wait_recv()
                for child, (there, device) in enumerate(targets):

                    @pl.when(there)
                    def _():
                        key_copy(k, c, child, device, key_ref, k * frame_rows).start()

        at = pl.ds(c * step_rows, step_rows)
        rows = normalise(own[at, :], gain_ref[...])
        q = jnp.dot(rows, wq[...], preferred_element_type=jnp.float32)
        q_ref[at, :] = (q * (HEAD_DIM ** (-0.5) * math.log2(math.e))).astype(jnp.bfloat16)
        k_ref[at, :] = jnp.dot(rows, wk[...], preferred_element_type=jnp.float32).astype(jnp.bfloat16)
        v_ref[at, :] = jnp.dot(rows, wv[...], preferred_element_type=jnp.float32).astype(jnp.bfloat16)

    for there, receives, remote, edge in halos:

        @pl.when(receives)
        def _():
            remote.wait_recv()

        @pl.when(jnp.logical_not(receives))
        def _():
            edge.wait()

        @pl.when(there)
        def _():
            remote.wait_send()

    for k in range(2):
        j, targets = children(k)

        @pl.when(j == 0)
        def _():
            pltpu.make_async_copy(
                tokens_ref.at[pl.ds(0, frame_rows), :],
                key_ref.at[pl.ds(k * frame_rows, frame_rows), :],
                root_sem.at[k],
            ).wait()

        for c in range(KEY_CHUNKS):
            for child, (there, device) in enumerate(targets):

                @pl.when(there)
                def _():
                    key_copy(k, c, child, device, key_ref, k * frame_rows).wait_send()


def exchange(token_rows, gain, query_weight, key_weight, value_weight, size, frame_rows):
    own_rows, width = token_rows.shape
    shape = lambda rows: jax.ShapeDtypeStruct((rows, width), jnp.bfloat16)
    hbm = pl.BlockSpec(memory_space=pl.ANY)
    vmem = pl.BlockSpec(memory_space=pltpu.VMEM)
    reach_rows = FRAME_REACH * frame_rows
    dma = pltpu.SemaphoreType.DMA
    square = pltpu.VMEM((width, width), jnp.bfloat16)
    return pl.pallas_call(
        functools.partial(exchange_kernel, size, frame_rows),
        out_shape=(
            shape(reach_rows), shape(reach_rows), shape(2 * frame_rows),
            shape(own_rows), shape(own_rows), shape(own_rows),
        ),
        in_specs=[hbm, vmem, hbm, hbm, hbm],
        out_specs=(hbm, hbm, hbm, vmem, vmem, vmem),
        scratch_shapes=[
            pltpu.VMEM((own_rows, width), jnp.bfloat16), square, square, square,
            dma((2,)), dma((2,)), dma((2, KEY_CHUNKS, 3)), dma((2, KEY_CHUNKS)),
            dma((4,)), dma((2,)), dma((2,)),
        ],
        compiler_params=pltpu.CompilerParams(
            collective_id=0, has_side_effects=True, vmem_limit_bytes=40 * 2 ** 20
        ),
    )(token_rows, gain, query_weight, key_weight, value_weight)


def fused(tokens, norm_gain, query_weight, key_weight, value_weight, out_weight, key_frames):
    frame_count, band_count, band_tokens, width_model = tokens.shape
    frame_rows = band_count * band_tokens
    keyframe_count = key_frames.shape[0]
    size = lax.axis_size("tm")
    me = lax.axis_index("tm")
    frames_total = size * frame_count
    token_rows = tokens.reshape(-1, width_model)
    gain = norm_gain.reshape(1, -1)
    left, right, key_tokens, queries, key_rows, values = exchange(
        token_rows, gain, query_weight, key_weight, value_weight, size, frame_rows
    )
    first_frame = me * frame_count
    frame_now = first_frame + jnp.arange(frame_count, dtype=jnp.int32)
    window = frame_now[:, None] - FRAME_REACH + jnp.arange(2 * FRAME_REACH + 1, dtype=jnp.int32)[None]
    valid = jnp.concatenate(
        [
            (window >= 0) & (window < frames_total),
            jnp.abs(frame_now[:, None] - key_frames[None]) > FRAME_REACH,
        ],
        axis=1,
    )
    group = 256
    ext_rows = (2 * FRAME_REACH + frame_count + keyframe_count) * frame_rows
    own_rows = frame_count * frame_rows
    whole = lambda shape: pl.BlockSpec(shape, lambda i: (0, 0), pipeline_mode=pl.Buffered(1))
    columns = pl.BlockSpec((width_model, group), lambda i: (0, i))
    own_columns = pl.BlockSpec((own_rows, group), lambda i: (0, i))
    out = pl.pallas_call(
        functools.partial(fused_kernel, frame_count, band_count, band_tokens, keyframe_count),
        grid=(width_model // group,),
        out_shape=jax.ShapeDtypeStruct((own_rows, width_model), jnp.bfloat16),
        in_specs=[
            pl.BlockSpec(memory_space=pltpu.SMEM),
            whole((FRAME_REACH * frame_rows, width_model)),
            whole((own_rows, width_model)),
            whole((FRAME_REACH * frame_rows, width_model)),
            whole((keyframe_count * frame_rows, width_model)),
            whole((1, width_model)),
            own_columns, own_columns, own_columns,
            columns, columns,
            whole((width_model, width_model)),
        ],
        out_specs=whole((own_rows, width_model)),
        scratch_shapes=[
            pltpu.VMEM((ext_rows, width_model), jnp.bfloat16),
            pltpu.VMEM((ext_rows, group), jnp.bfloat16),
            pltpu.VMEM((ext_rows, group), jnp.bfloat16),
            pltpu.VMEM((own_rows, width_model), jnp.bfloat16),
        ],
        compiler_params=pltpu.CompilerParams(vmem_limit_bytes=56 * 2 ** 20),
    )(
        valid.astype(jnp.int32),
        left, token_rows, right, key_tokens, gain,
        queries, key_rows, values, key_weight, value_weight, out_weight,
    )
    return out.reshape(tokens.shape)


def solution(mesh):
    simple = mesh.shape["band"] == 1 and mesh.shape["tm"] % 4 == 0

    def body(*args):
        frames, keys = args[0].shape[0], args[6].shape[0]
        if simple and frames >= FRAME_REACH and keys == 2:
            return fused(*args)
        return per_device(*args)

    in_specs = (P(("slab", "tm"), "band", None, None), P(), P(), P(), P(), P(), P("slab"))
    out_specs = P(("slab", "tm"), "band", None, None)
    return jax.shard_map(
        body, mesh=mesh, in_specs=in_specs, out_specs=out_specs, check_vma=False
    )
```

```python
import functools
import math

import jax
import jax.numpy as jnp
from jax import lax
from jax.experimental import pallas as pl
from jax.experimental.pallas import tpu as pltpu
from jax.sharding import PartitionSpec as P

HEAD_DIM = 64
FRAME_REACH = 2
BAND_REACH = 1


def padded(cells, sides, width):
    for axis, dim in sides:
        count = lax.axis_size(axis)
        ends = count - 1
        head = lax.slice_in_dim(cells, 0, width, axis=dim)
        tail = lax.slice_in_dim(cells, cells.shape[dim] - width, cells.shape[dim], axis=dim)
        cells = jnp.concatenate(
            [
                lax.ppermute(tail, axis, [(i, (i + 1) % count) for i in range(ends)]),
                cells,
                lax.ppermute(head, axis, [((i + 1) % count, i) for i in range(ends)]),
            ],
            axis=dim,
        )
    return cells


def from_root(array, axis, root):
    mine = lax.axis_index(axis) == root
    return lax.psum(jnp.where(mine, array, jnp.zeros_like(array)), axis)


def layer_norm(token_rows, norm_gain):
    rows_float = token_rows.astype(jnp.float32)
    centred = rows_float - jnp.mean(rows_float, axis=-1, keepdims=True)
    variance = jnp.mean(centred * centred, axis=-1, keepdims=True)
    return (centred * lax.rsqrt(variance + 1e-05) * norm_gain).astype(jnp.bfloat16)


def attend(queries, key_values, allowed, width_model):
    head_count = width_model // HEAD_DIM
    query_heads = queries.reshape(queries.shape[0], head_count, HEAD_DIM)
    key_heads = key_values[:, :width_model].reshape(-1, head_count, HEAD_DIM)
    value_heads = key_values[:, width_model:].reshape(-1, head_count, HEAD_DIM)
    scores = jnp.einsum(
        "qhd,khd->hqk", query_heads, key_heads, preferred_element_type=jnp.float32
    ) * HEAD_DIM ** (-0.5)
    scores = jnp.where(allowed[None, None, :], scores, jnp.float32(-1e30))
    largest = jnp.max(scores, axis=-1, keepdims=True)
    weights = jnp.exp(scores - largest)
    denominator = jnp.sum(weights, axis=-1)
    probs = weights.astype(jnp.bfloat16)
    context = jnp.einsum("hqk,khd->qhd", probs, value_heads, preferred_element_type=jnp.float32)
    context = context / jnp.transpose(denominator)[:, :, None]
    return context.reshape(queries.shape[0], width_model).astype(jnp.bfloat16)


def per_device(tokens, norm_gain, query_weight, key_weight, value_weight, out_weight, key_frames):
    frame_count, band_count, band_tokens, width_model = tokens.shape
    token_rows = tokens.reshape(-1, width_model)
    normed = layer_norm(token_rows, norm_gain)
    queries = jnp.dot(normed, query_weight, preferred_element_type=jnp.float32).astype(jnp.bfloat16)
    key_rows = jnp.dot(normed, key_weight, preferred_element_type=jnp.float32).astype(jnp.bfloat16)
    values = jnp.dot(normed, value_weight, preferred_element_type=jnp.float32).astype(jnp.bfloat16)
    queries = queries.reshape(frame_count, band_count, band_tokens, width_model)
    key_value = jnp.concatenate([key_rows, values], axis=1).reshape(
        frame_count, band_count, band_tokens, 2 * width_model
    )
    banded = padded(key_value, (("band", 1),), BAND_REACH)
    extended = padded(banded, (("tm", 0),), FRAME_REACH)
    first_frame = lax.axis_index("tm") * frame_count
    first_band = lax.axis_index("band") * band_count
    frames_total = lax.axis_size("tm") * frame_count
    bands_total = lax.axis_size("band") * band_count
    keyframe_count = key_frames.shape[0]

    def fetch(number, store):
        target = key_frames[number]
        owner = target // frame_count
        local = jnp.clip(target - first_frame, 0, frame_count - 1)
        candidate = lax.dynamic_index_in_dim(key_value, local, 0, keepdims=False)
        arrived = from_root(candidate, "tm", owner)
        return lax.dynamic_update_index_in_dim(store, arrived, number, 0)

    empty = jnp.zeros((keyframe_count, band_count, band_tokens, 2 * width_model), jnp.bfloat16)
    keyframe_store = lax.fori_loop(0, keyframe_count, fetch, empty)
    frame_span = 2 * FRAME_REACH + 1
    band_span = 2 * BAND_REACH + 1

    def one_block(number):
        frame_local = number // band_count
        band_local = number % band_count
        window = lax.dynamic_slice(
            extended,
            (frame_local, band_local, 0, 0),
            (frame_span, band_span, band_tokens, 2 * width_model),
        )
        frame_now = first_frame + frame_local
        band_now = first_band + band_local
        window_frame = frame_now - FRAME_REACH + jnp.arange(frame_span, dtype=jnp.int32)
        window_band = band_now - BAND_REACH + jnp.arange(band_span, dtype=jnp.int32)
        frame_valid = (window_frame >= 0) & (window_frame < frames_total)
        band_valid = (window_band >= 0) & (window_band < bands_total)
        allowed_window = jnp.broadcast_to(
            (frame_valid[:, None] & band_valid[None, :])[:, :, None],
            (frame_span, band_span, band_tokens),
        ).reshape(-1)
        allowed_keyframe = jnp.broadcast_to(
            (jnp.abs(frame_now - key_frames) > FRAME_REACH)[:, None], (keyframe_count, band_tokens)
        ).reshape(-1)
        allowed = jnp.concatenate([allowed_window, allowed_keyframe], axis=0)
        keyframe_band = lax.dynamic_index_in_dim(keyframe_store, band_local, 1, keepdims=False)
        key_values = jnp.concatenate(
            [window.reshape(-1, 2 * width_model), keyframe_band.reshape(-1, 2 * width_model)],
            axis=0,
        )
        block_queries = lax.dynamic_index_in_dim(
            lax.dynamic_index_in_dim(queries, frame_local, 0, keepdims=False),
            band_local,
            0,
            keepdims=False,
        )
        return attend(block_queries, key_values, allowed, width_model)

    context = lax.map(one_block, jnp.arange(frame_count * band_count, dtype=jnp.int32)).reshape(
        -1, width_model
    )
    updated = token_rows.astype(jnp.float32) + jnp.dot(
        context, out_weight, preferred_element_type=jnp.float32
    )
    return updated.astype(jnp.bfloat16).reshape(frame_count, band_count, band_tokens, width_model)


LANES = 128
NEG = -1e30


def fused_kernel(
    frames, bands, band_tokens, keys,
    valid_ref, left_ref, own_ref, right_ref, key_ref, gain_ref,
    q_ref, k_ref, v_ref, wk_ref, wv_ref, wo_ref, out_ref,
    normed, kbuf, vbuf, context,
):
    step = pl.program_id(0)
    group = wk_ref.shape[1]
    frame_rows = bands * band_tokens
    reach_rows = FRAME_REACH * frame_rows
    own_rows = frames * frame_rows
    sources = (
        (left_ref, 0, reach_rows),
        (right_ref, reach_rows + own_rows, reach_rows),
        (key_ref, 2 * reach_rows + own_rows, keys * frame_rows),
    )

    @pl.when(step == 0)
    def _():
        for source, base, count in sources:

            @pl.loop(0, count // LANES)
            def _(i):
                rows = source[pl.ds(pl.multiple_of(i * LANES, LANES), LANES), :]
                normed[pl.ds(pl.multiple_of(base + i * LANES, LANES), LANES), :] = normalise(rows, gain_ref[...])

    chunk = 512
    for _, base, count in sources:

        @pl.loop(0, count // chunk)
        def _(i):
            at = pl.ds(pl.multiple_of(base + i * chunk, chunk), chunk)
            rows = normed[at, :]
            kbuf[at, :] = jnp.dot(rows, wk_ref[...], preferred_element_type=jnp.float32).astype(jnp.bfloat16)
            vbuf[at, :] = jnp.dot(rows, wv_ref[...], preferred_element_type=jnp.float32).astype(jnp.bfloat16)

    kbuf[pl.ds(reach_rows, own_rows), :] = k_ref[...]
    vbuf[pl.ds(reach_rows, own_rows), :] = v_ref[...]

    span = 2 * FRAME_REACH + 1
    low = lax.broadcasted_iota(jnp.int32, (band_tokens, LANES), 1) < HEAD_DIM

    @pl.loop(0, frames * (group // LANES))
    def _(number):
        frame = number // (group // LANES)
        pair = number % (group // LANES)
        lanes = pl.ds(pl.multiple_of(pair * LANES, LANES), LANES)
        for band in range(bands):
            first = max(band - BAND_REACH, 0)
            count = min(band + BAND_REACH, bands - 1) + 1 - first
            at_q = pl.ds(pl.multiple_of(frame * frame_rows + band * band_tokens, band_tokens), band_tokens)
            q = q_ref[at_q, lanes]
            zero = jnp.zeros_like(q)
            q2 = jnp.concatenate([jnp.where(low, q, zero), jnp.where(low, zero, q)], axis=0)
            places = [
                pl.ds(
                    pl.multiple_of((frame + j) * frame_rows + first * band_tokens, band_tokens),
                    count * band_tokens,
                )
                for j in range(span)
            ] + [
                pl.ds(2 * reach_rows + own_rows + k * frame_rows + band * band_tokens, band_tokens)
                for k in range(keys)
            ]
            scores = []
            for j, place in enumerate(places):
                s = lax.dot_general(
                    q2, kbuf[place, lanes], (((1,), (1,)), ((), ())),
                    preferred_element_type=jnp.float32,
                )
                if j != FRAME_REACH:
                    s = jnp.where(valid_ref[frame, j] > 0, s, NEG)
                scores.append(s)
            largest = functools.reduce(
                jnp.maximum, [jnp.max(s, axis=-1, keepdims=True) for s in scores]
            )
            total = jnp.zeros((2 * band_tokens, LANES), jnp.float32)
            denominator = jnp.zeros((2 * band_tokens, 1), jnp.float32)
            for s, place in zip(scores, places):
                weights = jnp.exp2(s - largest)
                denominator += jnp.sum(weights, axis=-1, keepdims=True)
                total += jnp.dot(
                    weights.astype(jnp.bfloat16), vbuf[place, lanes],
                    preferred_element_type=jnp.float32,
                )
            total = total / denominator
            block = jnp.where(low, total[:band_tokens], total[band_tokens:])
            context[at_q, pl.ds(pl.multiple_of(step * group + pair * LANES, LANES), LANES)] = block.astype(
                jnp.bfloat16
            )

    @pl.when(step == pl.num_programs(0) - 1)
    def _():
        @pl.loop(0, own_rows // 256)
        def _(i):
            at = pl.ds(pl.multiple_of(i * 256, 256), 256)
            out_ref[at, :] = (
                own_ref[at, :].astype(jnp.float32)
                + jnp.dot(context[at, :], wo_ref[...], preferred_element_type=jnp.float32)
            ).astype(jnp.bfloat16)


KEY_CHUNKS = 4


def normalise(rows, gain):
    rows = rows.astype(jnp.float32)
    centred = rows - jnp.mean(rows, axis=-1, keepdims=True)
    variance = jnp.mean(centred * centred, axis=-1, keepdims=True)
    return (centred * lax.rsqrt(variance + 1e-05) * gain).astype(jnp.bfloat16)


def exchange_kernel(
    size, frame_rows,
    tokens_ref, gain_ref, wq_hbm, wk_hbm, wv_hbm,
    left_ref, right_ref, key_ref, q_ref, k_ref, v_ref,
    own, wq, wk, wv, halo_send, halo_recv, key_send, key_recv, local_sem, edge_sem, root_sem,
):
    me = lax.axis_index("tm")
    place = lax.rem(me, 4)
    own_rows = tokens_ref.shape[0]
    reach_rows = FRAME_REACH * frame_rows
    across = jnp.where(place < 2, me + 2, me - 2)
    corner = (place == 0) | (place == 3)
    partners = (
        (me > 0, me - 1),
        (me < size - 1, me + 1),
        (me >= 0, across),
        (corner & (me >= 4), me - 4),
        (corner & (me < size - 4), me + 4),
    )
    barrier = pltpu.get_barrier_semaphore()
    expected = 0
    for there, device in partners:
        expected = expected + jnp.where(there, 1, 0)

        @pl.when(there)
        def _():
            pl.semaphore_signal(
                barrier, inc=1, device_id={"tm": device}, device_id_type=pl.DeviceIdType.MESH
            )

    pl.semaphore_wait(barrier, expected)

    part = frame_rows // KEY_CHUNKS

    def children(k):
        j = me if k == 0 else size - 1 - me
        sign = 1 if k == 0 else -1
        r = lax.rem(j, 4)
        return j, (
            ((r == 0) & (j < size - 4), me + 4 * sign),
            (r == 0, me + 2 * sign),
            (lax.rem(j, 2) == 0, me + sign),
        )

    def key_copy(k, c, child, device, source, base):
        return pltpu.make_async_remote_copy(
            src_ref=source.at[pl.ds(base + c * part, part), :],
            dst_ref=key_ref.at[pl.ds(k * frame_rows + c * part, part), :],
            send_sem=key_send.at[k, c, child],
            recv_sem=key_recv.at[k, c],
            device_id={"tm": device},
            device_id_type=pl.DeviceIdType.MESH,
        )

    for k in range(2):
        j, targets = children(k)
        base = 0 if k == 0 else own_rows - frame_rows

        @pl.when(j == 0)
        def _():
            for c in range(KEY_CHUNKS):
                for child, (there, device) in enumerate(targets):
                    key_copy(k, c, child, device, tokens_ref, base).start()
            pltpu.make_async_copy(
                tokens_ref.at[pl.ds(base, frame_rows), :],
                key_ref.at[pl.ds(k * frame_rows, frame_rows), :],
                root_sem.at[k],
            ).start()

    halos = []
    for side, (there, device, base, target) in enumerate((
        (me < size - 1, me + 1, own_rows - reach_rows, left_ref),
        (me > 0, me - 1, 0, right_ref),
    )):
        remote = pltpu.make_async_remote_copy(
            src_ref=tokens_ref.at[pl.ds(base, reach_rows), :],
            dst_ref=target,
            send_sem=halo_send.at[side],
            recv_sem=halo_recv.at[side],
            device_id={"tm": device},
            device_id_type=pl.DeviceIdType.MESH,
        )
        edge = pltpu.make_async_copy(
            tokens_ref.at[pl.ds(base, reach_rows), :], target, edge_sem.at[side]
        )
        receives = me > 0 if side == 0 else me < size - 1
        halos.append((there, receives, remote, edge))

        @pl.when(there)
        def _():
            remote.start()

        @pl.when(jnp.logical_not(receives))
        def _():
            edge.start()

    loads = [
        pltpu.make_async_copy(source, target, local_sem.at[i])
        for i, (source, target) in enumerate(
            ((tokens_ref, own), (wq_hbm, wq), (wk_hbm, wk), (wv_hbm, wv))
        )
    ]
    for load in loads:
        load.start()
    for load in loads:
        load.wait()

    def forward(k, c):
        j, targets = children(k)

        @pl.when(j > 0)
        def _():
            key_copy(k, c, 0, across, key_ref, k * frame_rows).wait_recv()
            for child, (there, device) in enumerate(targets):

                @pl.when(there)
                def _():
                    key_copy(k, c, child, device, key_ref, k * frame_rows).start()

    near_first = me < size // 2

    @pl.when(near_first)
    def _():
        for c in range(KEY_CHUNKS):
            forward(0, c)

    @pl.when(jnp.logical_not(near_first))
    def _():
        for c in range(KEY_CHUNKS):
            forward(1, c)

    step_rows = own_rows // KEY_CHUNKS
    for c in range(KEY_CHUNKS):

        @pl.when(near_first)
        def _():
            forward(1, c)

        @pl.when(jnp.logical_not(near_first))
        def _():
            forward(0, c)

        at = pl.ds(c * step_rows, step_rows)
        rows = normalise(own[at, :], gain_ref[...])
        q = jnp.dot(rows, wq[...], preferred_element_type=jnp.float32)
        q_ref[at, :] = (q * (HEAD_DIM ** (-0.5) * math.log2(math.e))).astype(jnp.bfloat16)
        k_ref[at, :] = jnp.dot(rows, wk[...], preferred_element_type=jnp.float32).astype(jnp.bfloat16)
        v_ref[at, :] = jnp.dot(rows, wv[...], preferred_element_type=jnp.float32).astype(jnp.bfloat16)

    for there, receives, remote, edge in halos:

        @pl.when(receives)
        def _():
            remote.wait_recv()

        @pl.when(jnp.logical_not(receives))
        def _():
            edge.wait()

        @pl.when(there)
        def _():
            remote.wait_send()

    for k in range(2):
        j, targets = children(k)

        @pl.when(j == 0)
        def _():
            pltpu.make_async_copy(
                tokens_ref.at[pl.ds(0, frame_rows), :],
                key_ref.at[pl.ds(k * frame_rows, frame_rows), :],
                root_sem.at[k],
            ).wait()

        for c in range(KEY_CHUNKS):
            for child, (there, device) in enumerate(targets):

                @pl.when(there)
                def _():
                    key_copy(k, c, child, device, key_ref, k * frame_rows).wait_send()


def exchange(token_rows, gain, query_weight, key_weight, value_weight, size, frame_rows):
    own_rows, width = token_rows.shape
    shape = lambda rows: jax.ShapeDtypeStruct((rows, width), jnp.bfloat16)
    hbm = pl.BlockSpec(memory_space=pl.ANY)
    vmem = pl.BlockSpec(memory_space=pltpu.VMEM)
    reach_rows = FRAME_REACH * frame_rows
    dma = pltpu.SemaphoreType.DMA
    square = pltpu.VMEM((width, width), jnp.bfloat16)
    return pl.pallas_call(
        functools.partial(exchange_kernel, size, frame_rows),
        out_shape=(
            shape(reach_rows), shape(reach_rows), shape(2 * frame_rows),
            shape(own_rows), shape(own_rows), shape(own_rows),
        ),
        in_specs=[hbm, vmem, hbm, hbm, hbm],
        out_specs=(hbm, hbm, hbm, vmem, vmem, vmem),
        scratch_shapes=[
            pltpu.VMEM((own_rows, width), jnp.bfloat16), square, square, square,
            dma((2,)), dma((2,)), dma((2, KEY_CHUNKS, 3)), dma((2, KEY_CHUNKS)),
            dma((4,)), dma((2,)), dma((2,)),
        ],
        compiler_params=pltpu.CompilerParams(
            collective_id=0, has_side_effects=True, vmem_limit_bytes=40 * 2 ** 20
        ),
    )(token_rows, gain, query_weight, key_weight, value_weight)


def fused(tokens, norm_gain, query_weight, key_weight, value_weight, out_weight, key_frames):
    frame_count, band_count, band_tokens, width_model = tokens.shape
    frame_rows = band_count * band_tokens
    keyframe_count = key_frames.shape[0]
    size = lax.axis_size("tm")
    me = lax.axis_index("tm")
    frames_total = size * frame_count
    token_rows = tokens.reshape(-1, width_model)
    gain = norm_gain.reshape(1, -1)
    left, right, key_tokens, queries, key_rows, values = exchange(
        token_rows, gain, query_weight, key_weight, value_weight, size, frame_rows
    )
    first_frame = me * frame_count
    frame_now = first_frame + jnp.arange(frame_count, dtype=jnp.int32)
    window = frame_now[:, None] - FRAME_REACH + jnp.arange(2 * FRAME_REACH + 1, dtype=jnp.int32)[None]
    valid = jnp.concatenate(
        [
            (window >= 0) & (window < frames_total),
            jnp.abs(frame_now[:, None] - key_frames[None]) > FRAME_REACH,
        ],
        axis=1,
    )
    group = 256
    ext_rows = (2 * FRAME_REACH + frame_count + keyframe_count) * frame_rows
    own_rows = frame_count * frame_rows
    whole = lambda shape: pl.BlockSpec(shape, lambda i: (0, 0), pipeline_mode=pl.Buffered(1))
    columns = pl.BlockSpec((width_model, group), lambda i: (0, i))
    own_columns = pl.BlockSpec((own_rows, group), lambda i: (0, i))
    out = pl.pallas_call(
        functools.partial(fused_kernel, frame_count, band_count, band_tokens, keyframe_count),
        grid=(width_model // group,),
        out_shape=jax.ShapeDtypeStruct((own_rows, width_model), jnp.bfloat16),
        in_specs=[
            pl.BlockSpec(memory_space=pltpu.SMEM),
            whole((FRAME_REACH * frame_rows, width_model)),
            whole((own_rows, width_model)),
            whole((FRAME_REACH * frame_rows, width_model)),
            whole((keyframe_count * frame_rows, width_model)),
            whole((1, width_model)),
            own_columns, own_columns, own_columns,
            columns, columns,
            whole((width_model, width_model)),
        ],
        out_specs=whole((own_rows, width_model)),
        scratch_shapes=[
            pltpu.VMEM((ext_rows, width_model), jnp.bfloat16),
            pltpu.VMEM((ext_rows, group), jnp.bfloat16),
            pltpu.VMEM((ext_rows, group), jnp.bfloat16),
            pltpu.VMEM((own_rows, width_model), jnp.bfloat16),
        ],
        compiler_params=pltpu.CompilerParams(vmem_limit_bytes=56 * 2 ** 20),
    )(
        valid.astype(jnp.int32),
        left, token_rows, right, key_tokens, gain,
        queries, key_rows, values, key_weight, value_weight, out_weight,
    )
    return out.reshape(tokens.shape)


def solution(mesh):
    simple = mesh.shape["band"] == 1 and mesh.shape["tm"] % 4 == 0

    def body(*args):
        frames, keys = args[0].shape[0], args[6].shape[0]
        if simple and frames >= FRAME_REACH and keys == 2:
            return fused(*args)
        return per_device(*args)

    in_specs = (P(("slab", "tm"), "band", None, None), P(), P(), P(), P(), P(), P("slab"))
    out_specs = P(("slab", "tm"), "band", None, None)
    return jax.shard_map(
        body, mesh=mesh, in_specs=in_specs, out_specs=out_specs, check_vma=False
    )
```

```python
import functools
import math

import jax
import jax.numpy as jnp
from jax import lax
from jax.experimental import pallas as pl
from jax.experimental.pallas import tpu as pltpu
from jax.sharding import PartitionSpec as P

HEAD_DIM = 64
FRAME_REACH = 2
BAND_REACH = 1


def padded(cells, sides, width):
    for axis, dim in sides:
        count = lax.axis_size(axis)
        ends = count - 1
        head = lax.slice_in_dim(cells, 0, width, axis=dim)
        tail = lax.slice_in_dim(cells, cells.shape[dim] - width, cells.shape[dim], axis=dim)
        cells = jnp.concatenate(
            [
                lax.ppermute(tail, axis, [(i, (i + 1) % count) for i in range(ends)]),
                cells,
                lax.ppermute(head, axis, [((i + 1) % count, i) for i in range(ends)]),
            ],
            axis=dim,
        )
    return cells


def from_root(array, axis, root):
    mine = lax.axis_index(axis) == root
    return lax.psum(jnp.where(mine, array, jnp.zeros_like(array)), axis)


def layer_norm(token_rows, norm_gain):
    rows_float = token_rows.astype(jnp.float32)
    centred = rows_float - jnp.mean(rows_float, axis=-1, keepdims=True)
    variance = jnp.mean(centred * centred, axis=-1, keepdims=True)
    return (centred * lax.rsqrt(variance + 1e-05) * norm_gain).astype(jnp.bfloat16)


def attend(queries, key_values, allowed, width_model):
    head_count = width_model // HEAD_DIM
    query_heads = queries.reshape(queries.shape[0], head_count, HEAD_DIM)
    key_heads = key_values[:, :width_model].reshape(-1, head_count, HEAD_DIM)
    value_heads = key_values[:, width_model:].reshape(-1, head_count, HEAD_DIM)
    scores = jnp.einsum(
        "qhd,khd->hqk", query_heads, key_heads, preferred_element_type=jnp.float32
    ) * HEAD_DIM ** (-0.5)
    scores = jnp.where(allowed[None, None, :], scores, jnp.float32(-1e30))
    largest = jnp.max(scores, axis=-1, keepdims=True)
    weights = jnp.exp(scores - largest)
    denominator = jnp.sum(weights, axis=-1)
    probs = weights.astype(jnp.bfloat16)
    context = jnp.einsum("hqk,khd->qhd", probs, value_heads, preferred_element_type=jnp.float32)
    context = context / jnp.transpose(denominator)[:, :, None]
    return context.reshape(queries.shape[0], width_model).astype(jnp.bfloat16)


def per_device(tokens, norm_gain, query_weight, key_weight, value_weight, out_weight, key_frames):
    frame_count, band_count, band_tokens, width_model = tokens.shape
    token_rows = tokens.reshape(-1, width_model)
    normed = layer_norm(token_rows, norm_gain)
    queries = jnp.dot(normed, query_weight, preferred_element_type=jnp.float32).astype(jnp.bfloat16)
    key_rows = jnp.dot(normed, key_weight, preferred_element_type=jnp.float32).astype(jnp.bfloat16)
    values = jnp.dot(normed, value_weight, preferred_element_type=jnp.float32).astype(jnp.bfloat16)
    queries = queries.reshape(frame_count, band_count, band_tokens, width_model)
    key_value = jnp.concatenate([key_rows, values], axis=1).reshape(
        frame_count, band_count, band_tokens, 2 * width_model
    )
    banded = padded(key_value, (("band", 1),), BAND_REACH)
    extended = padded(banded, (("tm", 0),), FRAME_REACH)
    first_frame = lax.axis_index("tm") * frame_count
    first_band = lax.axis_index("band") * band_count
    frames_total = lax.axis_size("tm") * frame_count
    bands_total = lax.axis_size("band") * band_count
    keyframe_count = key_frames.shape[0]

    def fetch(number, store):
        target = key_frames[number]
        owner = target // frame_count
        local = jnp.clip(target - first_frame, 0, frame_count - 1)
        candidate = lax.dynamic_index_in_dim(key_value, local, 0, keepdims=False)
        arrived = from_root(candidate, "tm", owner)
        return lax.dynamic_update_index_in_dim(store, arrived, number, 0)

    empty = jnp.zeros((keyframe_count, band_count, band_tokens, 2 * width_model), jnp.bfloat16)
    keyframe_store = lax.fori_loop(0, keyframe_count, fetch, empty)
    frame_span = 2 * FRAME_REACH + 1
    band_span = 2 * BAND_REACH + 1

    def one_block(number):
        frame_local = number // band_count
        band_local = number % band_count
        window = lax.dynamic_slice(
            extended,
            (frame_local, band_local, 0, 0),
            (frame_span, band_span, band_tokens, 2 * width_model),
        )
        frame_now = first_frame + frame_local
        band_now = first_band + band_local
        window_frame = frame_now - FRAME_REACH + jnp.arange(frame_span, dtype=jnp.int32)
        window_band = band_now - BAND_REACH + jnp.arange(band_span, dtype=jnp.int32)
        frame_valid = (window_frame >= 0) & (window_frame < frames_total)
        band_valid = (window_band >= 0) & (window_band < bands_total)
        allowed_window = jnp.broadcast_to(
            (frame_valid[:, None] & band_valid[None, :])[:, :, None],
            (frame_span, band_span, band_tokens),
        ).reshape(-1)
        allowed_keyframe = jnp.broadcast_to(
            (jnp.abs(frame_now - key_frames) > FRAME_REACH)[:, None], (keyframe_count, band_tokens)
        ).reshape(-1)
        allowed = jnp.concatenate([allowed_window, allowed_keyframe], axis=0)
        keyframe_band = lax.dynamic_index_in_dim(keyframe_store, band_local, 1, keepdims=False)
        key_values = jnp.concatenate(
            [window.reshape(-1, 2 * width_model), keyframe_band.reshape(-1, 2 * width_model)],
            axis=0,
        )
        block_queries = lax.dynamic_index_in_dim(
            lax.dynamic_index_in_dim(queries, frame_local, 0, keepdims=False),
            band_local,
            0,
            keepdims=False,
        )
        return attend(block_queries, key_values, allowed, width_model)

    context = lax.map(one_block, jnp.arange(frame_count * band_count, dtype=jnp.int32)).reshape(
        -1, width_model
    )
    updated = token_rows.astype(jnp.float32) + jnp.dot(
        context, out_weight, preferred_element_type=jnp.float32
    )
    return updated.astype(jnp.bfloat16).reshape(frame_count, band_count, band_tokens, width_model)


LANES = 128
NEG = -1e30


def fused_kernel(
    frames, bands, band_tokens, keys,
    valid_ref, left_ref, own_ref, right_ref, key_ref, gain_ref,
    q_ref, k_ref, v_ref, wk_ref, wv_ref, wo_ref, out_ref,
    normed, kbuf, vbuf, context,
):
    step = pl.program_id(0)
    group = wk_ref.shape[1]
    frame_rows = bands * band_tokens
    reach_rows = FRAME_REACH * frame_rows
    own_rows = frames * frame_rows
    sources = (
        (left_ref, 0, reach_rows),
        (right_ref, reach_rows + own_rows, reach_rows),
        (key_ref, 2 * reach_rows + own_rows, keys * frame_rows),
    )

    @pl.when(step == 0)
    def _():
        for source, base, count in sources:

            @pl.loop(0, count // LANES)
            def _(i):
                rows = source[pl.ds(pl.multiple_of(i * LANES, LANES), LANES), :]
                normed[pl.ds(pl.multiple_of(base + i * LANES, LANES), LANES), :] = normalise(rows, gain_ref[...])

    chunk = 512
    for _, base, count in sources:

        @pl.loop(0, count // chunk)
        def _(i):
            at = pl.ds(pl.multiple_of(base + i * chunk, chunk), chunk)
            rows = normed[at, :]
            kbuf[at, :] = jnp.dot(rows, wk_ref[...], preferred_element_type=jnp.float32).astype(jnp.bfloat16)
            vbuf[at, :] = jnp.dot(rows, wv_ref[...], preferred_element_type=jnp.float32).astype(jnp.bfloat16)

    kbuf[pl.ds(reach_rows, own_rows), :] = k_ref[...]
    vbuf[pl.ds(reach_rows, own_rows), :] = v_ref[...]

    span = 2 * FRAME_REACH + 1
    low = lax.broadcasted_iota(jnp.int32, (band_tokens, LANES), 1) < HEAD_DIM

    @pl.loop(0, frames * (group // LANES))
    def _(number):
        frame = number // (group // LANES)
        pair = number % (group // LANES)
        lanes = pl.ds(pl.multiple_of(pair * LANES, LANES), LANES)
        for band in range(bands):
            first = max(band - BAND_REACH, 0)
            count = min(band + BAND_REACH, bands - 1) + 1 - first
            at_q = pl.ds(pl.multiple_of(frame * frame_rows + band * band_tokens, band_tokens), band_tokens)
            q = q_ref[at_q, lanes]
            zero = jnp.zeros_like(q)
            q2 = jnp.concatenate([jnp.where(low, q, zero), jnp.where(low, zero, q)], axis=0)
            places = [
                pl.ds(
                    pl.multiple_of((frame + j) * frame_rows + first * band_tokens, band_tokens),
                    count * band_tokens,
                )
                for j in range(span)
            ] + [
                pl.ds(2 * reach_rows + own_rows + k * frame_rows + band * band_tokens, band_tokens)
                for k in range(keys)
            ]
            scores = []
            for j, place in enumerate(places):
                s = lax.dot_general(
                    q2, kbuf[place, lanes], (((1,), (1,)), ((), ())),
                    preferred_element_type=jnp.float32,
                )
                if j != FRAME_REACH:
                    s = jnp.where(valid_ref[frame, j] > 0, s, NEG)
                scores.append(s)
            split = lambda s: [s[:, i : i + LANES] for i in range(0, s.shape[1], LANES)]
            largest = jnp.max(
                functools.reduce(jnp.maximum, sum([split(s) for s in scores], [])),
                axis=-1, keepdims=True,
            )
            total = jnp.zeros((2 * band_tokens, LANES), jnp.float32)
            lane_sums = jnp.zeros((2 * band_tokens, LANES), jnp.float32)
            for s, place in zip(scores, places):
                weights = jnp.exp2(s - largest)
                lane_sums += functools.reduce(jnp.add, split(weights))
                total += jnp.dot(
                    weights.astype(jnp.bfloat16), vbuf[place, lanes],
                    preferred_element_type=jnp.float32,
                )
            denominator = jnp.sum(lane_sums, axis=-1, keepdims=True)
            block = jnp.where(low, total[:band_tokens], total[band_tokens:]) / jnp.where(
                low, denominator[:band_tokens], denominator[band_tokens:]
            )
            context[at_q, pl.ds(pl.multiple_of(step * group + pair * LANES, LANES), LANES)] = block.astype(
                jnp.bfloat16
            )

    @pl.when(step == pl.num_programs(0) - 1)
    def _():
        @pl.loop(0, own_rows // 256)
        def _(i):
            at = pl.ds(pl.multiple_of(i * 256, 256), 256)
            out_ref[at, :] = (
                own_ref[at, :].astype(jnp.float32)
                + jnp.dot(context[at, :], wo_ref[...], preferred_element_type=jnp.float32)
            ).astype(jnp.bfloat16)


KEY_CHUNKS = 4


def normalise(rows, gain):
    rows = rows.astype(jnp.float32)
    centred = rows - jnp.mean(rows, axis=-1, keepdims=True)
    variance = jnp.mean(centred * centred, axis=-1, keepdims=True)
    return (centred * lax.rsqrt(variance + 1e-05) * gain).astype(jnp.bfloat16)


def exchange_kernel(
    size, frame_rows,
    tokens_ref, gain_ref, wq_hbm, wk_hbm, wv_hbm,
    left_ref, right_ref, key_ref, q_ref, k_ref, v_ref,
    own, wq, wk, wv, halo_send, halo_recv, key_send, key_recv, local_sem, edge_sem, root_sem,
):
    me = lax.axis_index("tm")
    place = lax.rem(me, 4)
    own_rows = tokens_ref.shape[0]
    reach_rows = FRAME_REACH * frame_rows
    across = jnp.where(place < 2, me + 2, me - 2)
    partners = (
        (me > 0, me - 1),
        (me < size - 1, me + 1),
        (me >= 0, across),
        (me >= 4, me - 4),
        (me < size - 4, me + 4),
    )
    barrier = pltpu.get_barrier_semaphore()
    expected = 0
    for there, device in partners:
        expected = expected + jnp.where(there, 1, 0)

        @pl.when(there)
        def _():
            pl.semaphore_signal(
                barrier, inc=1, device_id={"tm": device}, device_id_type=pl.DeviceIdType.MESH
            )

    pl.semaphore_wait(barrier, expected)

    part = frame_rows // KEY_CHUNKS

    def children(k):
        j = me if k == 0 else size - 1 - me
        sign = 1 if k == 0 else -1
        return j, (
            ((lax.rem(j, 2) == 0) & (j < size - 4), me + 4 * sign),
            (j == 0, me + 2 * sign),
            (lax.rem(j, 2) == 0, me + sign),
        )

    def key_copy(k, c, child, device, source, base):
        return pltpu.make_async_remote_copy(
            src_ref=source.at[pl.ds(base + c * part, part), :],
            dst_ref=key_ref.at[pl.ds(k * frame_rows + c * part, part), :],
            send_sem=key_send.at[k, c, child],
            recv_sem=key_recv.at[k, c],
            device_id={"tm": device},
            device_id_type=pl.DeviceIdType.MESH,
        )

    for k in range(2):
        j, targets = children(k)
        base = 0 if k == 0 else own_rows - frame_rows

        @pl.when(j == 0)
        def _():
            for c in range(KEY_CHUNKS):
                for child, (there, device) in enumerate(targets):
                    key_copy(k, c, child, device, tokens_ref, base).start()
            pltpu.make_async_copy(
                tokens_ref.at[pl.ds(base, frame_rows), :],
                key_ref.at[pl.ds(k * frame_rows, frame_rows), :],
                root_sem.at[k],
            ).start()

    halos = []
    for side, (there, device, base, target) in enumerate((
        (me < size - 1, me + 1, own_rows - reach_rows, left_ref),
        (me > 0, me - 1, 0, right_ref),
    )):
        remote = pltpu.make_async_remote_copy(
            src_ref=tokens_ref.at[pl.ds(base, reach_rows), :],
            dst_ref=target,
            send_sem=halo_send.at[side],
            recv_sem=halo_recv.at[side],
            device_id={"tm": device},
            device_id_type=pl.DeviceIdType.MESH,
        )
        edge = pltpu.make_async_copy(
            tokens_ref.at[pl.ds(base, reach_rows), :], target, edge_sem.at[side]
        )
        receives = me > 0 if side == 0 else me < size - 1
        halos.append((there, receives, remote, edge))

        @pl.when(there)
        def _():
            remote.start()

        @pl.when(jnp.logical_not(receives))
        def _():
            edge.start()

    loads = [
        pltpu.make_async_copy(source, target, local_sem.at[i])
        for i, (source, target) in enumerate(
            ((tokens_ref, own), (wq_hbm, wq), (wk_hbm, wk), (wv_hbm, wv))
        )
    ]
    for load in loads:
        load.start()
    for load in loads:
        load.wait()

    def forward(k, c):
        j, targets = children(k)

        @pl.when(j > 0)
        def _():
            key_copy(k, c, 0, across, key_ref, k * frame_rows).wait_recv()
            for child, (there, device) in enumerate(targets):

                @pl.when(there)
                def _():
                    key_copy(k, c, child, device, key_ref, k * frame_rows).start()

    near_first = me < size // 2

    @pl.when(near_first)
    def _():
        for c in range(KEY_CHUNKS):
            forward(0, c)

    @pl.when(jnp.logical_not(near_first))
    def _():
        for c in range(KEY_CHUNKS):
            forward(1, c)

    step_rows = own_rows // KEY_CHUNKS
    for c in range(KEY_CHUNKS):

        @pl.when(near_first)
        def _():
            forward(1, c)

        @pl.when(jnp.logical_not(near_first))
        def _():
            forward(0, c)

        at = pl.ds(c * step_rows, step_rows)
        rows = normalise(own[at, :], gain_ref[...])
        q = jnp.dot(rows, wq[...], preferred_element_type=jnp.float32)
        q_ref[at, :] = (q * (HEAD_DIM ** (-0.5) * math.log2(math.e))).astype(jnp.bfloat16)
        k_ref[at, :] = jnp.dot(rows, wk[...], preferred_element_type=jnp.float32).astype(jnp.bfloat16)
        v_ref[at, :] = jnp.dot(rows, wv[...], preferred_element_type=jnp.float32).astype(jnp.bfloat16)

    for there, receives, remote, edge in halos:

        @pl.when(receives)
        def _():
            remote.wait_recv()

        @pl.when(jnp.logical_not(receives))
        def _():
            edge.wait()

        @pl.when(there)
        def _():
            remote.wait_send()

    for k in range(2):
        j, targets = children(k)

        @pl.when(j == 0)
        def _():
            pltpu.make_async_copy(
                tokens_ref.at[pl.ds(0, frame_rows), :],
                key_ref.at[pl.ds(k * frame_rows, frame_rows), :],
                root_sem.at[k],
            ).wait()

        for c in range(KEY_CHUNKS):
            for child, (there, device) in enumerate(targets):

                @pl.when(there)
                def _():
                    key_copy(k, c, child, device, key_ref, k * frame_rows).wait_send()


def exchange(token_rows, gain, query_weight, key_weight, value_weight, size, frame_rows):
    own_rows, width = token_rows.shape
    shape = lambda rows: jax.ShapeDtypeStruct((rows, width), jnp.bfloat16)
    hbm = pl.BlockSpec(memory_space=pl.ANY)
    vmem = pl.BlockSpec(memory_space=pltpu.VMEM)
    reach_rows = FRAME_REACH * frame_rows
    dma = pltpu.SemaphoreType.DMA
    square = pltpu.VMEM((width, width), jnp.bfloat16)
    return pl.pallas_call(
        functools.partial(exchange_kernel, size, frame_rows),
        out_shape=(
            shape(reach_rows), shape(reach_rows), shape(2 * frame_rows),
            shape(own_rows), shape(own_rows), shape(own_rows),
        ),
        in_specs=[hbm, vmem, hbm, hbm, hbm],
        out_specs=(hbm, hbm, hbm, vmem, vmem, vmem),
        scratch_shapes=[
            pltpu.VMEM((own_rows, width), jnp.bfloat16), square, square, square,
            dma((2,)), dma((2,)), dma((2, KEY_CHUNKS, 3)), dma((2, KEY_CHUNKS)),
            dma((4,)), dma((2,)), dma((2,)),
        ],
        compiler_params=pltpu.CompilerParams(
            collective_id=0, has_side_effects=True, vmem_limit_bytes=40 * 2 ** 20
        ),
    )(token_rows, gain, query_weight, key_weight, value_weight)


def fused(tokens, norm_gain, query_weight, key_weight, value_weight, out_weight, key_frames):
    frame_count, band_count, band_tokens, width_model = tokens.shape
    frame_rows = band_count * band_tokens
    keyframe_count = key_frames.shape[0]
    size = lax.axis_size("tm")
    me = lax.axis_index("tm")
    frames_total = size * frame_count
    token_rows = tokens.reshape(-1, width_model)
    gain = norm_gain.reshape(1, -1)
    left, right, key_tokens, queries, key_rows, values = exchange(
        token_rows, gain, query_weight, key_weight, value_weight, size, frame_rows
    )
    first_frame = me * frame_count
    frame_now = first_frame + jnp.arange(frame_count, dtype=jnp.int32)
    window = frame_now[:, None] - FRAME_REACH + jnp.arange(2 * FRAME_REACH + 1, dtype=jnp.int32)[None]
    valid = jnp.concatenate(
        [
            (window >= 0) & (window < frames_total),
            jnp.abs(frame_now[:, None] - key_frames[None]) > FRAME_REACH,
        ],
        axis=1,
    )
    group = 256
    ext_rows = (2 * FRAME_REACH + frame_count + keyframe_count) * frame_rows
    own_rows = frame_count * frame_rows
    whole = lambda shape: pl.BlockSpec(shape, lambda i: (0, 0), pipeline_mode=pl.Buffered(1))
    columns = pl.BlockSpec((width_model, group), lambda i: (0, i))
    own_columns = pl.BlockSpec((own_rows, group), lambda i: (0, i))
    out = pl.pallas_call(
        functools.partial(fused_kernel, frame_count, band_count, band_tokens, keyframe_count),
        grid=(width_model // group,),
        out_shape=jax.ShapeDtypeStruct((own_rows, width_model), jnp.bfloat16),
        in_specs=[
            pl.BlockSpec(memory_space=pltpu.SMEM),
            whole((FRAME_REACH * frame_rows, width_model)),
            whole((own_rows, width_model)),
            whole((FRAME_REACH * frame_rows, width_model)),
            whole((keyframe_count * frame_rows, width_model)),
            whole((1, width_model)),
            own_columns, own_columns, own_columns,
            columns, columns,
            whole((width_model, width_model)),
        ],
        out_specs=whole((own_rows, width_model)),
        scratch_shapes=[
            pltpu.VMEM((ext_rows, width_model), jnp.bfloat16),
            pltpu.VMEM((ext_rows, group), jnp.bfloat16),
            pltpu.VMEM((ext_rows, group), jnp.bfloat16),
            pltpu.VMEM((own_rows, width_model), jnp.bfloat16),
        ],
        compiler_params=pltpu.CompilerParams(vmem_limit_bytes=56 * 2 ** 20),
    )(
        valid.astype(jnp.int32),
        left, token_rows, right, key_tokens, gain,
        queries, key_rows, values, key_weight, value_weight, out_weight,
    )
    return out.reshape(tokens.shape)


def solution(mesh):
    simple = mesh.shape["band"] == 1 and mesh.shape["tm"] % 4 == 0

    def body(*args):
        frames, keys = args[0].shape[0], args[6].shape[0]
        if simple and frames >= FRAME_REACH and keys == 2:
            return fused(*args)
        return per_device(*args)

    in_specs = (P(("slab", "tm"), "band", None, None), P(), P(), P(), P(), P(), P("slab"))
    out_specs = P(("slab", "tm"), "band", None, None)
    return jax.shard_map(
        body, mesh=mesh, in_specs=in_specs, out_specs=out_specs, check_vma=False
    )
```

```python
import functools
import math

import jax
import jax.numpy as jnp
from jax import lax
from jax.experimental import pallas as pl
from jax.experimental.pallas import tpu as pltpu
from jax.sharding import PartitionSpec as P

HEAD_DIM = 64
FRAME_REACH = 2
BAND_REACH = 1


def padded(cells, sides, width):
    for axis, dim in sides:
        count = lax.axis_size(axis)
        ends = count - 1
        head = lax.slice_in_dim(cells, 0, width, axis=dim)
        tail = lax.slice_in_dim(cells, cells.shape[dim] - width, cells.shape[dim], axis=dim)
        cells = jnp.concatenate(
            [
                lax.ppermute(tail, axis, [(i, (i + 1) % count) for i in range(ends)]),
                cells,
                lax.ppermute(head, axis, [((i + 1) % count, i) for i in range(ends)]),
            ],
            axis=dim,
        )
    return cells


def from_root(array, axis, root):
    mine = lax.axis_index(axis) == root
    return lax.psum(jnp.where(mine, array, jnp.zeros_like(array)), axis)


def layer_norm(token_rows, norm_gain):
    rows_float = token_rows.astype(jnp.float32)
    centred = rows_float - jnp.mean(rows_float, axis=-1, keepdims=True)
    variance = jnp.mean(centred * centred, axis=-1, keepdims=True)
    return (centred * lax.rsqrt(variance + 1e-05) * norm_gain).astype(jnp.bfloat16)


def attend(queries, key_values, allowed, width_model):
    head_count = width_model // HEAD_DIM
    query_heads = queries.reshape(queries.shape[0], head_count, HEAD_DIM)
    key_heads = key_values[:, :width_model].reshape(-1, head_count, HEAD_DIM)
    value_heads = key_values[:, width_model:].reshape(-1, head_count, HEAD_DIM)
    scores = jnp.einsum(
        "qhd,khd->hqk", query_heads, key_heads, preferred_element_type=jnp.float32
    ) * HEAD_DIM ** (-0.5)
    scores = jnp.where(allowed[None, None, :], scores, jnp.float32(-1e30))
    largest = jnp.max(scores, axis=-1, keepdims=True)
    weights = jnp.exp(scores - largest)
    denominator = jnp.sum(weights, axis=-1)
    probs = weights.astype(jnp.bfloat16)
    context = jnp.einsum("hqk,khd->qhd", probs, value_heads, preferred_element_type=jnp.float32)
    context = context / jnp.transpose(denominator)[:, :, None]
    return context.reshape(queries.shape[0], width_model).astype(jnp.bfloat16)


def per_device(tokens, norm_gain, query_weight, key_weight, value_weight, out_weight, key_frames):
    frame_count, band_count, band_tokens, width_model = tokens.shape
    token_rows = tokens.reshape(-1, width_model)
    normed = layer_norm(token_rows, norm_gain)
    queries = jnp.dot(normed, query_weight, preferred_element_type=jnp.float32).astype(jnp.bfloat16)
    key_rows = jnp.dot(normed, key_weight, preferred_element_type=jnp.float32).astype(jnp.bfloat16)
    values = jnp.dot(normed, value_weight, preferred_element_type=jnp.float32).astype(jnp.bfloat16)
    queries = queries.reshape(frame_count, band_count, band_tokens, width_model)
    key_value = jnp.concatenate([key_rows, values], axis=1).reshape(
        frame_count, band_count, band_tokens, 2 * width_model
    )
    banded = padded(key_value, (("band", 1),), BAND_REACH)
    extended = padded(banded, (("tm", 0),), FRAME_REACH)
    first_frame = lax.axis_index("tm") * frame_count
    first_band = lax.axis_index("band") * band_count
    frames_total = lax.axis_size("tm") * frame_count
    bands_total = lax.axis_size("band") * band_count
    keyframe_count = key_frames.shape[0]

    def fetch(number, store):
        target = key_frames[number]
        owner = target // frame_count
        local = jnp.clip(target - first_frame, 0, frame_count - 1)
        candidate = lax.dynamic_index_in_dim(key_value, local, 0, keepdims=False)
        arrived = from_root(candidate, "tm", owner)
        return lax.dynamic_update_index_in_dim(store, arrived, number, 0)

    empty = jnp.zeros((keyframe_count, band_count, band_tokens, 2 * width_model), jnp.bfloat16)
    keyframe_store = lax.fori_loop(0, keyframe_count, fetch, empty)
    frame_span = 2 * FRAME_REACH + 1
    band_span = 2 * BAND_REACH + 1

    def one_block(number):
        frame_local = number // band_count
        band_local = number % band_count
        window = lax.dynamic_slice(
            extended,
            (frame_local, band_local, 0, 0),
            (frame_span, band_span, band_tokens, 2 * width_model),
        )
        frame_now = first_frame + frame_local
        band_now = first_band + band_local
        window_frame = frame_now - FRAME_REACH + jnp.arange(frame_span, dtype=jnp.int32)
        window_band = band_now - BAND_REACH + jnp.arange(band_span, dtype=jnp.int32)
        frame_valid = (window_frame >= 0) & (window_frame < frames_total)
        band_valid = (window_band >= 0) & (window_band < bands_total)
        allowed_window = jnp.broadcast_to(
            (frame_valid[:, None] & band_valid[None, :])[:, :, None],
            (frame_span, band_span, band_tokens),
        ).reshape(-1)
        allowed_keyframe = jnp.broadcast_to(
            (jnp.abs(frame_now - key_frames) > FRAME_REACH)[:, None], (keyframe_count, band_tokens)
        ).reshape(-1)
        allowed = jnp.concatenate([allowed_window, allowed_keyframe], axis=0)
        keyframe_band = lax.dynamic_index_in_dim(keyframe_store, band_local, 1, keepdims=False)
        key_values = jnp.concatenate(
            [window.reshape(-1, 2 * width_model), keyframe_band.reshape(-1, 2 * width_model)],
            axis=0,
        )
        block_queries = lax.dynamic_index_in_dim(
            lax.dynamic_index_in_dim(queries, frame_local, 0, keepdims=False),
            band_local,
            0,
            keepdims=False,
        )
        return attend(block_queries, key_values, allowed, width_model)

    context = lax.map(one_block, jnp.arange(frame_count * band_count, dtype=jnp.int32)).reshape(
        -1, width_model
    )
    updated = token_rows.astype(jnp.float32) + jnp.dot(
        context, out_weight, preferred_element_type=jnp.float32
    )
    return updated.astype(jnp.bfloat16).reshape(frame_count, band_count, band_tokens, width_model)


LANES = 128
NEG = -1e30


def fused_kernel(
    frames, bands, band_tokens, keys,
    valid_ref, left_ref, own_ref, right_ref, key_ref, gain_ref,
    q_ref, k_ref, v_ref, wk_ref, wv_ref, wo_ref, out_ref,
    normed, kbuf, vbuf, context,
):
    step = pl.program_id(0)
    group = wk_ref.shape[1]
    frame_rows = bands * band_tokens
    reach_rows = FRAME_REACH * frame_rows
    own_rows = frames * frame_rows
    sources = (
        (left_ref, 0, reach_rows),
        (right_ref, reach_rows + own_rows, reach_rows),
        (key_ref, 2 * reach_rows + own_rows, keys * frame_rows),
    )

    @pl.when(step == 0)
    def _():
        for source, base, count in sources:

            @pl.loop(0, count // LANES)
            def _(i):
                rows = source[pl.ds(pl.multiple_of(i * LANES, LANES), LANES), :]
                normed[pl.ds(pl.multiple_of(base + i * LANES, LANES), LANES), :] = normalise(rows, gain_ref[...])

    chunk = 512
    for _, base, count in sources:

        @pl.loop(0, count // chunk)
        def _(i):
            at = pl.ds(pl.multiple_of(base + i * chunk, chunk), chunk)
            rows = normed[at, :]
            kbuf[at, :] = jnp.dot(rows, wk_ref[...], preferred_element_type=jnp.float32).astype(jnp.bfloat16)
            vbuf[at, :] = jnp.dot(rows, wv_ref[...], preferred_element_type=jnp.float32).astype(jnp.bfloat16)

    kbuf[pl.ds(reach_rows, own_rows), :] = k_ref[...]
    vbuf[pl.ds(reach_rows, own_rows), :] = v_ref[...]

    span = 2 * FRAME_REACH + 1
    low = lax.broadcasted_iota(jnp.int32, (band_tokens, LANES), 1) < HEAD_DIM

    @pl.loop(0, frames * (group // LANES))
    def _(number):
        frame = number // (group // LANES)
        pair = number % (group // LANES)
        lanes = pl.ds(pl.multiple_of(pair * LANES, LANES), LANES)
        for band in range(bands):
            first = max(band - BAND_REACH, 0)
            count = min(band + BAND_REACH, bands - 1) + 1 - first
            at_q = pl.ds(pl.multiple_of(frame * frame_rows + band * band_tokens, band_tokens), band_tokens)
            q = q_ref[at_q, lanes]
            zero = jnp.zeros_like(q)
            q2 = jnp.concatenate([jnp.where(low, q, zero), jnp.where(low, zero, q)], axis=0)
            places = [
                pl.ds(
                    pl.multiple_of((frame + j) * frame_rows + first * band_tokens, band_tokens),
                    count * band_tokens,
                )
                for j in range(span)
            ] + [
                pl.ds(2 * reach_rows + own_rows + k * frame_rows + band * band_tokens, band_tokens)
                for k in range(keys)
            ]
            scores = []
            for j, place in enumerate(places):
                s = lax.dot_general(
                    q2, kbuf[place, lanes], (((1,), (1,)), ((), ())),
                    preferred_element_type=jnp.float32,
                )
                if j != FRAME_REACH:
                    s = jnp.where(valid_ref[frame, j] > 0, s, NEG)
                scores.append(s)
            split = lambda s: [s[:, i : i + LANES] for i in range(0, s.shape[1], LANES)]
            largest = jnp.max(
                functools.reduce(jnp.maximum, sum([split(s) for s in scores], [])),
                axis=-1, keepdims=True,
            )
            total = jnp.zeros((2 * band_tokens, LANES), jnp.float32)
            lane_sums = jnp.zeros((2 * band_tokens, LANES), jnp.float32)
            for s, place in zip(scores, places):
                weights = jnp.exp2(s - largest)
                lane_sums += functools.reduce(jnp.add, split(weights))
                total += jnp.dot(
                    weights.astype(jnp.bfloat16), vbuf[place, lanes],
                    preferred_element_type=jnp.float32,
                )
            denominator = jnp.sum(lane_sums, axis=-1, keepdims=True)
            block = jnp.where(low, total[:band_tokens], total[band_tokens:]) / jnp.where(
                low, denominator[:band_tokens], denominator[band_tokens:]
            )
            context[at_q, pl.ds(pl.multiple_of(step * group + pair * LANES, LANES), LANES)] = block.astype(
                jnp.bfloat16
            )

    @pl.when(step == pl.num_programs(0) - 1)
    def _():
        @pl.loop(0, own_rows // 256)
        def _(i):
            at = pl.ds(pl.multiple_of(i * 256, 256), 256)
            out_ref[at, :] = (
                own_ref[at, :].astype(jnp.float32)
                + jnp.dot(context[at, :], wo_ref[...], preferred_element_type=jnp.float32)
            ).astype(jnp.bfloat16)


KEY_CHUNKS = 8
PROJECTIONS = 4


def normalise(rows, gain):
    rows = rows.astype(jnp.float32)
    centred = rows - jnp.mean(rows, axis=-1, keepdims=True)
    variance = jnp.mean(centred * centred, axis=-1, keepdims=True)
    return (centred * lax.rsqrt(variance + 1e-05) * gain).astype(jnp.bfloat16)


def exchange_kernel(
    size, frame_rows,
    tokens_ref, gain_ref, wq_hbm, wk_hbm, wv_hbm,
    left_ref, right_ref, key_ref, q_ref, k_ref, v_ref,
    own, wq, wk, wv, halo_send, halo_recv, key_send, key_recv, local_sem, edge_sem, root_sem,
):
    me = lax.axis_index("tm")
    place = lax.rem(me, 4)
    own_rows = tokens_ref.shape[0]
    reach_rows = FRAME_REACH * frame_rows
    across = jnp.where(place < 2, me + 2, me - 2)
    partners = (
        (me > 0, me - 1),
        (me < size - 1, me + 1),
        (me >= 0, across),
        (me >= 4, me - 4),
        (me < size - 4, me + 4),
    )
    barrier = pltpu.get_barrier_semaphore()
    expected = 0
    for there, device in partners:
        expected = expected + jnp.where(there, 1, 0)

        @pl.when(there)
        def _():
            pl.semaphore_signal(
                barrier, inc=1, device_id={"tm": device}, device_id_type=pl.DeviceIdType.MESH
            )

    pl.semaphore_wait(barrier, expected)

    part = frame_rows // KEY_CHUNKS

    def children(k):
        j = me if k == 0 else size - 1 - me
        sign = 1 if k == 0 else -1
        return j, (
            ((lax.rem(j, 2) == 0) & (j < size - 4), me + 4 * sign),
            (j == 0, me + 2 * sign),
            (lax.rem(j, 2) == 0, me + sign),
        )

    def key_copy(k, c, child, device, source, base):
        return pltpu.make_async_remote_copy(
            src_ref=source.at[pl.ds(base + c * part, part), :],
            dst_ref=key_ref.at[pl.ds(k * frame_rows + c * part, part), :],
            send_sem=key_send.at[k, c, child],
            recv_sem=key_recv.at[k, c],
            device_id={"tm": device},
            device_id_type=pl.DeviceIdType.MESH,
        )

    for k in range(2):
        j, targets = children(k)
        base = 0 if k == 0 else own_rows - frame_rows

        @pl.when(j == 0)
        def _():
            for c in range(KEY_CHUNKS):
                for child, (there, device) in enumerate(targets):
                    key_copy(k, c, child, device, tokens_ref, base).start()
            pltpu.make_async_copy(
                tokens_ref.at[pl.ds(base, frame_rows), :],
                key_ref.at[pl.ds(k * frame_rows, frame_rows), :],
                root_sem.at[k],
            ).start()

    halos = []
    for side, (there, device, base, target) in enumerate((
        (me < size - 1, me + 1, own_rows - reach_rows, left_ref),
        (me > 0, me - 1, 0, right_ref),
    )):
        remote = pltpu.make_async_remote_copy(
            src_ref=tokens_ref.at[pl.ds(base, reach_rows), :],
            dst_ref=target,
            send_sem=halo_send.at[side],
            recv_sem=halo_recv.at[side],
            device_id={"tm": device},
            device_id_type=pl.DeviceIdType.MESH,
        )
        edge = pltpu.make_async_copy(
            tokens_ref.at[pl.ds(base, reach_rows), :], target, edge_sem.at[side]
        )
        receives = me > 0 if side == 0 else me < size - 1
        halos.append((there, receives, remote, edge))

        @pl.when(there)
        def _():
            remote.start()

        @pl.when(jnp.logical_not(receives))
        def _():
            edge.start()

    loads = [
        pltpu.make_async_copy(source, target, local_sem.at[i])
        for i, (source, target) in enumerate(
            ((tokens_ref, own), (wq_hbm, wq), (wk_hbm, wk), (wv_hbm, wv))
        )
    ]
    for load in loads:
        load.start()
    for load in loads:
        load.wait()

    def forward(k, c):
        j, targets = children(k)

        @pl.when(j > 0)
        def _():
            key_copy(k, c, 0, across, key_ref, k * frame_rows).wait_recv()
            for child, (there, device) in enumerate(targets):

                @pl.when(there)
                def _():
                    key_copy(k, c, child, device, key_ref, k * frame_rows).start()

    near_first = me < size // 2

    @pl.when(near_first)
    def _():
        for c in range(KEY_CHUNKS):
            forward(0, c)

    @pl.when(jnp.logical_not(near_first))
    def _():
        for c in range(KEY_CHUNKS):
            forward(1, c)

    step_rows = own_rows // PROJECTIONS
    every = KEY_CHUNKS // PROJECTIONS
    for c in range(KEY_CHUNKS):

        @pl.when(near_first)
        def _():
            forward(1, c)

        @pl.when(jnp.logical_not(near_first))
        def _():
            forward(0, c)

        if c % every != every - 1:
            continue
        at = pl.ds(c // every * step_rows, step_rows)
        rows = normalise(own[at, :], gain_ref[...])
        q = jnp.dot(rows, wq[...], preferred_element_type=jnp.float32)
        q_ref[at, :] = (q * (HEAD_DIM ** (-0.5) * math.log2(math.e))).astype(jnp.bfloat16)
        k_ref[at, :] = jnp.dot(rows, wk[...], preferred_element_type=jnp.float32).astype(jnp.bfloat16)
        v_ref[at, :] = jnp.dot(rows, wv[...], preferred_element_type=jnp.float32).astype(jnp.bfloat16)

    for there, receives, remote, edge in halos:

        @pl.when(receives)
        def _():
            remote.wait_recv()

        @pl.when(jnp.logical_not(receives))
        def _():
            edge.wait()

        @pl.when(there)
        def _():
            remote.wait_send()

    for k in range(2):
        j, targets = children(k)

        @pl.when(j == 0)
        def _():
            pltpu.make_async_copy(
                tokens_ref.at[pl.ds(0, frame_rows), :],
                key_ref.at[pl.ds(k * frame_rows, frame_rows), :],
                root_sem.at[k],
            ).wait()

        for c in range(KEY_CHUNKS):
            for child, (there, device) in enumerate(targets):

                @pl.when(there)
                def _():
                    key_copy(k, c, child, device, key_ref, k * frame_rows).wait_send()


def exchange(token_rows, gain, query_weight, key_weight, value_weight, size, frame_rows):
    own_rows, width = token_rows.shape
    shape = lambda rows: jax.ShapeDtypeStruct((rows, width), jnp.bfloat16)
    hbm = pl.BlockSpec(memory_space=pl.ANY)
    vmem = pl.BlockSpec(memory_space=pltpu.VMEM)
    reach_rows = FRAME_REACH * frame_rows
    dma = pltpu.SemaphoreType.DMA
    square = pltpu.VMEM((width, width), jnp.bfloat16)
    return pl.pallas_call(
        functools.partial(exchange_kernel, size, frame_rows),
        out_shape=(
            shape(reach_rows), shape(reach_rows), shape(2 * frame_rows),
            shape(own_rows), shape(own_rows), shape(own_rows),
        ),
        in_specs=[hbm, vmem, hbm, hbm, hbm],
        out_specs=(hbm, hbm, hbm, vmem, vmem, vmem),
        scratch_shapes=[
            pltpu.VMEM((own_rows, width), jnp.bfloat16), square, square, square,
            dma((2,)), dma((2,)), dma((2, KEY_CHUNKS, 3)), dma((2, KEY_CHUNKS)),
            dma((4,)), dma((2,)), dma((2,)),
        ],
        compiler_params=pltpu.CompilerParams(
            collective_id=0, has_side_effects=True, vmem_limit_bytes=40 * 2 ** 20
        ),
    )(token_rows, gain, query_weight, key_weight, value_weight)


def fused(tokens, norm_gain, query_weight, key_weight, value_weight, out_weight, key_frames):
    frame_count, band_count, band_tokens, width_model = tokens.shape
    frame_rows = band_count * band_tokens
    keyframe_count = key_frames.shape[0]
    size = lax.axis_size("tm")
    me = lax.axis_index("tm")
    frames_total = size * frame_count
    token_rows = tokens.reshape(-1, width_model)
    gain = norm_gain.reshape(1, -1)
    left, right, key_tokens, queries, key_rows, values = exchange(
        token_rows, gain, query_weight, key_weight, value_weight, size, frame_rows
    )
    first_frame = me * frame_count
    frame_now = first_frame + jnp.arange(frame_count, dtype=jnp.int32)
    window = frame_now[:, None] - FRAME_REACH + jnp.arange(2 * FRAME_REACH + 1, dtype=jnp.int32)[None]
    valid = jnp.concatenate(
        [
            (window >= 0) & (window < frames_total),
            jnp.abs(frame_now[:, None] - key_frames[None]) > FRAME_REACH,
        ],
        axis=1,
    )
    group = 256
    ext_rows = (2 * FRAME_REACH + frame_count + keyframe_count) * frame_rows
    own_rows = frame_count * frame_rows
    whole = lambda shape: pl.BlockSpec(shape, lambda i: (0, 0), pipeline_mode=pl.Buffered(1))
    columns = pl.BlockSpec((width_model, group), lambda i: (0, i))
    own_columns = pl.BlockSpec((own_rows, group), lambda i: (0, i))
    out = pl.pallas_call(
        functools.partial(fused_kernel, frame_count, band_count, band_tokens, keyframe_count),
        grid=(width_model // group,),
        out_shape=jax.ShapeDtypeStruct((own_rows, width_model), jnp.bfloat16),
        in_specs=[
            pl.BlockSpec(memory_space=pltpu.SMEM),
            whole((FRAME_REACH * frame_rows, width_model)),
            whole((own_rows, width_model)),
            whole((FRAME_REACH * frame_rows, width_model)),
            whole((keyframe_count * frame_rows, width_model)),
            whole((1, width_model)),
            own_columns, own_columns, own_columns,
            columns, columns,
            whole((width_model, width_model)),
        ],
        out_specs=whole((own_rows, width_model)),
        scratch_shapes=[
            pltpu.VMEM((ext_rows, width_model), jnp.bfloat16),
            pltpu.VMEM((ext_rows, group), jnp.bfloat16),
            pltpu.VMEM((ext_rows, group), jnp.bfloat16),
            pltpu.VMEM((own_rows, width_model), jnp.bfloat16),
        ],
        compiler_params=pltpu.CompilerParams(vmem_limit_bytes=56 * 2 ** 20),
    )(
        valid.astype(jnp.int32),
        left, token_rows, right, key_tokens, gain,
        queries, key_rows, values, key_weight, value_weight, out_weight,
    )
    return out.reshape(tokens.shape)


def solution(mesh):
    simple = mesh.shape["band"] == 1 and mesh.shape["tm"] % 4 == 0

    def body(*args):
        frames, keys = args[0].shape[0], args[6].shape[0]
        if simple and frames >= FRAME_REACH and keys == 2:
            return fused(*args)
        return per_device(*args)

    in_specs = (P(("slab", "tm"), "band", None, None), P(), P(), P(), P(), P(), P("slab"))
    out_specs = P(("slab", "tm"), "band", None, None)
    return jax.shard_map(
        body, mesh=mesh, in_specs=in_specs, out_specs=out_specs, check_vma=False
    )
```

```python
import functools
import math

import jax
import jax.numpy as jnp
from jax import lax
from jax.experimental import pallas as pl
from jax.experimental.pallas import tpu as pltpu
from jax.sharding import PartitionSpec as P

HEAD_DIM = 64
FRAME_REACH = 2
BAND_REACH = 1


def padded(cells, sides, width):
    for axis, dim in sides:
        count = lax.axis_size(axis)
        ends = count - 1
        head = lax.slice_in_dim(cells, 0, width, axis=dim)
        tail = lax.slice_in_dim(cells, cells.shape[dim] - width, cells.shape[dim], axis=dim)
        cells = jnp.concatenate(
            [
                lax.ppermute(tail, axis, [(i, (i + 1) % count) for i in range(ends)]),
                cells,
                lax.ppermute(head, axis, [((i + 1) % count, i) for i in range(ends)]),
            ],
            axis=dim,
        )
    return cells


def from_root(array, axis, root):
    mine = lax.axis_index(axis) == root
    return lax.psum(jnp.where(mine, array, jnp.zeros_like(array)), axis)


def layer_norm(token_rows, norm_gain):
    rows_float = token_rows.astype(jnp.float32)
    centred = rows_float - jnp.mean(rows_float, axis=-1, keepdims=True)
    variance = jnp.mean(centred * centred, axis=-1, keepdims=True)
    return (centred * lax.rsqrt(variance + 1e-05) * norm_gain).astype(jnp.bfloat16)


def attend(queries, key_values, allowed, width_model):
    head_count = width_model // HEAD_DIM
    query_heads = queries.reshape(queries.shape[0], head_count, HEAD_DIM)
    key_heads = key_values[:, :width_model].reshape(-1, head_count, HEAD_DIM)
    value_heads = key_values[:, width_model:].reshape(-1, head_count, HEAD_DIM)
    scores = jnp.einsum(
        "qhd,khd->hqk", query_heads, key_heads, preferred_element_type=jnp.float32
    ) * HEAD_DIM ** (-0.5)
    scores = jnp.where(allowed[None, None, :], scores, jnp.float32(-1e30))
    largest = jnp.max(scores, axis=-1, keepdims=True)
    weights = jnp.exp(scores - largest)
    denominator = jnp.sum(weights, axis=-1)
    probs = weights.astype(jnp.bfloat16)
    context = jnp.einsum("hqk,khd->qhd", probs, value_heads, preferred_element_type=jnp.float32)
    context = context / jnp.transpose(denominator)[:, :, None]
    return context.reshape(queries.shape[0], width_model).astype(jnp.bfloat16)


def per_device(tokens, norm_gain, query_weight, key_weight, value_weight, out_weight, key_frames):
    frame_count, band_count, band_tokens, width_model = tokens.shape
    token_rows = tokens.reshape(-1, width_model)
    normed = layer_norm(token_rows, norm_gain)
    queries = jnp.dot(normed, query_weight, preferred_element_type=jnp.float32).astype(jnp.bfloat16)
    key_rows = jnp.dot(normed, key_weight, preferred_element_type=jnp.float32).astype(jnp.bfloat16)
    values = jnp.dot(normed, value_weight, preferred_element_type=jnp.float32).astype(jnp.bfloat16)
    queries = queries.reshape(frame_count, band_count, band_tokens, width_model)
    key_value = jnp.concatenate([key_rows, values], axis=1).reshape(
        frame_count, band_count, band_tokens, 2 * width_model
    )
    banded = padded(key_value, (("band", 1),), BAND_REACH)
    extended = padded(banded, (("tm", 0),), FRAME_REACH)
    first_frame = lax.axis_index("tm") * frame_count
    first_band = lax.axis_index("band") * band_count
    frames_total = lax.axis_size("tm") * frame_count
    bands_total = lax.axis_size("band") * band_count
    keyframe_count = key_frames.shape[0]

    def fetch(number, store):
        target = key_frames[number]
        owner = target // frame_count
        local = jnp.clip(target - first_frame, 0, frame_count - 1)
        candidate = lax.dynamic_index_in_dim(key_value, local, 0, keepdims=False)
        arrived = from_root(candidate, "tm", owner)
        return lax.dynamic_update_index_in_dim(store, arrived, number, 0)

    empty = jnp.zeros((keyframe_count, band_count, band_tokens, 2 * width_model), jnp.bfloat16)
    keyframe_store = lax.fori_loop(0, keyframe_count, fetch, empty)
    frame_span = 2 * FRAME_REACH + 1
    band_span = 2 * BAND_REACH + 1

    def one_block(number):
        frame_local = number // band_count
        band_local = number % band_count
        window = lax.dynamic_slice(
            extended,
            (frame_local, band_local, 0, 0),
            (frame_span, band_span, band_tokens, 2 * width_model),
        )
        frame_now = first_frame + frame_local
        band_now = first_band + band_local
        window_frame = frame_now - FRAME_REACH + jnp.arange(frame_span, dtype=jnp.int32)
        window_band = band_now - BAND_REACH + jnp.arange(band_span, dtype=jnp.int32)
        frame_valid = (window_frame >= 0) & (window_frame < frames_total)
        band_valid = (window_band >= 0) & (window_band < bands_total)
        allowed_window = jnp.broadcast_to(
            (frame_valid[:, None] & band_valid[None, :])[:, :, None],
            (frame_span, band_span, band_tokens),
        ).reshape(-1)
        allowed_keyframe = jnp.broadcast_to(
            (jnp.abs(frame_now - key_frames) > FRAME_REACH)[:, None], (keyframe_count, band_tokens)
        ).reshape(-1)
        allowed = jnp.concatenate([allowed_window, allowed_keyframe], axis=0)
        keyframe_band = lax.dynamic_index_in_dim(keyframe_store, band_local, 1, keepdims=False)
        key_values = jnp.concatenate(
            [window.reshape(-1, 2 * width_model), keyframe_band.reshape(-1, 2 * width_model)],
            axis=0,
        )
        block_queries = lax.dynamic_index_in_dim(
            lax.dynamic_index_in_dim(queries, frame_local, 0, keepdims=False),
            band_local,
            0,
            keepdims=False,
        )
        return attend(block_queries, key_values, allowed, width_model)

    context = lax.map(one_block, jnp.arange(frame_count * band_count, dtype=jnp.int32)).reshape(
        -1, width_model
    )
    updated = token_rows.astype(jnp.float32) + jnp.dot(
        context, out_weight, preferred_element_type=jnp.float32
    )
    return updated.astype(jnp.bfloat16).reshape(frame_count, band_count, band_tokens, width_model)


LANES = 128
NEG = -1e30


def fused_kernel(
    frames, bands, band_tokens, keys,
    valid_ref, left_ref, own_ref, right_ref, key_ref, gain_ref,
    q_ref, k_ref, v_ref, wk_ref, wv_ref, wo_ref, out_ref,
    normed, kbuf, vbuf, context,
):
    step = pl.program_id(0)
    group = wk_ref.shape[1]
    frame_rows = bands * band_tokens
    reach_rows = FRAME_REACH * frame_rows
    own_rows = frames * frame_rows
    sources = (
        (left_ref, 0, reach_rows),
        (right_ref, reach_rows + own_rows, reach_rows),
        (key_ref, 2 * reach_rows + own_rows, keys * frame_rows),
    )

    @pl.when(step == 0)
    def _():
        for source, base, count in sources:

            @pl.loop(0, count // LANES)
            def _(i):
                rows = source[pl.ds(pl.multiple_of(i * LANES, LANES), LANES), :]
                normed[pl.ds(pl.multiple_of(base + i * LANES, LANES), LANES), :] = normalise(rows, gain_ref[...])

    chunk = 512
    for _, base, count in sources:

        @pl.loop(0, count // chunk)
        def _(i):
            at = pl.ds(pl.multiple_of(base + i * chunk, chunk), chunk)
            rows = normed[at, :]
            kbuf[at, :] = jnp.dot(rows, wk_ref[...], preferred_element_type=jnp.float32).astype(jnp.bfloat16)
            vbuf[at, :] = jnp.dot(rows, wv_ref[...], preferred_element_type=jnp.float32).astype(jnp.bfloat16)

    kbuf[pl.ds(reach_rows, own_rows), :] = k_ref[...]
    vbuf[pl.ds(reach_rows, own_rows), :] = v_ref[...]

    span = 2 * FRAME_REACH + 1
    low = lax.broadcasted_iota(jnp.int32, (band_tokens, LANES), 1) < HEAD_DIM

    @pl.loop(0, frames * (group // LANES))
    def _(number):
        frame = number // (group // LANES)
        pair = number % (group // LANES)
        lanes = pl.ds(pl.multiple_of(pair * LANES, LANES), LANES)
        for band in range(bands):
            first = max(band - BAND_REACH, 0)
            count = min(band + BAND_REACH, bands - 1) + 1 - first
            at_q = pl.ds(pl.multiple_of(frame * frame_rows + band * band_tokens, band_tokens), band_tokens)
            q = q_ref[at_q, lanes]
            zero = jnp.zeros_like(q)
            q2 = jnp.concatenate([jnp.where(low, q, zero), jnp.where(low, zero, q)], axis=0)
            places = [
                pl.ds(
                    pl.multiple_of((frame + j) * frame_rows + first * band_tokens, band_tokens),
                    count * band_tokens,
                )
                for j in range(span)
            ] + [
                pl.ds(2 * reach_rows + own_rows + k * frame_rows + band * band_tokens, band_tokens)
                for k in range(keys)
            ]
            scores = []
            for j, place in enumerate(places):
                s = lax.dot_general(
                    q2, kbuf[place, lanes], (((1,), (1,)), ((), ())),
                    preferred_element_type=jnp.float32,
                )
                if j != FRAME_REACH:
                    s = jnp.where(valid_ref[frame, j] > 0, s, NEG)
                scores.append(s)
            split = lambda s: [s[:, i : i + LANES] for i in range(0, s.shape[1], LANES)]
            largest = jnp.max(
                functools.reduce(jnp.maximum, sum([split(s) for s in scores], [])),
                axis=-1, keepdims=True,
            )
            total = jnp.zeros((2 * band_tokens, LANES), jnp.float32)
            lane_sums = jnp.zeros((2 * band_tokens, LANES), jnp.float32)
            for s, place in zip(scores, places):
                weights = jnp.exp2(s - largest)
                lane_sums += functools.reduce(jnp.add, split(weights))
                total += jnp.dot(
                    weights.astype(jnp.bfloat16), vbuf[place, lanes],
                    preferred_element_type=jnp.float32,
                )
            denominator = jnp.sum(lane_sums, axis=-1, keepdims=True)
            block = jnp.where(low, total[:band_tokens], total[band_tokens:]) / jnp.where(
                low, denominator[:band_tokens], denominator[band_tokens:]
            )
            context[at_q, pl.ds(pl.multiple_of(step * group + pair * LANES, LANES), LANES)] = block.astype(
                jnp.bfloat16
            )

    @pl.when(step == pl.num_programs(0) - 1)
    def _():
        @pl.loop(0, own_rows // 256)
        def _(i):
            at = pl.ds(pl.multiple_of(i * 256, 256), 256)
            out_ref[at, :] = (
                own_ref[at, :].astype(jnp.float32)
                + jnp.dot(context[at, :], wo_ref[...], preferred_element_type=jnp.float32)
            ).astype(jnp.bfloat16)


KEY_CHUNKS = 8
PROJECTIONS = 4


def normalise(rows, gain):
    rows = rows.astype(jnp.float32)
    centred = rows - jnp.mean(rows, axis=-1, keepdims=True)
    variance = jnp.mean(centred * centred, axis=-1, keepdims=True)
    return (centred * lax.rsqrt(variance + 1e-05) * gain).astype(jnp.bfloat16)


def exchange_kernel(
    size, frame_rows,
    tokens_ref, gain_ref, wq_hbm, wk_hbm, wv_hbm,
    left_ref, right_ref, key_ref, q_ref, k_ref, v_ref,
    own, wq, wk, wv, halo_send, halo_recv, key_send, key_recv, local_sem, edge_sem, root_sem,
):
    me = lax.axis_index("tm")
    place = lax.rem(me, 4)
    own_rows = tokens_ref.shape[0]
    reach_rows = FRAME_REACH * frame_rows
    across = jnp.where(place < 2, me + 2, me - 2)
    partners = (
        (me > 0, me - 1),
        (me < size - 1, me + 1),
        (me >= 0, across),
        (me >= 4, me - 4),
        (me < size - 4, me + 4),
    )
    barrier = pltpu.get_barrier_semaphore()
    expected = 0
    for there, device in partners:
        expected = expected + jnp.where(there, 1, 0)

        @pl.when(there)
        def _():
            pl.semaphore_signal(
                barrier, inc=1, device_id={"tm": device}, device_id_type=pl.DeviceIdType.MESH
            )

    pl.semaphore_wait(barrier, expected)

    part = frame_rows // KEY_CHUNKS

    def children(k):
        j = me if k == 0 else size - 1 - me
        sign = 1 if k == 0 else -1
        return j, (
            ((lax.rem(j, 2) == 0) & (j < size - 4), me + 4 * sign),
            (j == 0, me + 2 * sign),
            (lax.rem(j, 2) == 0, me + sign),
        )

    def key_copy(k, c, child, device, source, base):
        return pltpu.make_async_remote_copy(
            src_ref=source.at[pl.ds(base + c * part, part), :],
            dst_ref=key_ref.at[pl.ds(k * frame_rows + c * part, part), :],
            send_sem=key_send.at[k, c, child],
            recv_sem=key_recv.at[k, c],
            device_id={"tm": device},
            device_id_type=pl.DeviceIdType.MESH,
        )

    for k in range(2):
        j, targets = children(k)
        base = 0 if k == 0 else own_rows - frame_rows

        @pl.when(j == 0)
        def _():
            for c in range(KEY_CHUNKS):
                for child, (there, device) in enumerate(targets):
                    key_copy(k, c, child, device, tokens_ref, base).start()
            pltpu.make_async_copy(
                tokens_ref.at[pl.ds(base, frame_rows), :],
                key_ref.at[pl.ds(k * frame_rows, frame_rows), :],
                root_sem.at[k],
            ).start()

    halos = []
    for side, (there, device, base, target) in enumerate((
        (me < size - 1, me + 1, own_rows - reach_rows, left_ref),
        (me > 0, me - 1, 0, right_ref),
    )):
        remote = pltpu.make_async_remote_copy(
            src_ref=tokens_ref.at[pl.ds(base, reach_rows), :],
            dst_ref=target,
            send_sem=halo_send.at[side],
            recv_sem=halo_recv.at[side],
            device_id={"tm": device},
            device_id_type=pl.DeviceIdType.MESH,
        )
        edge = pltpu.make_async_copy(
            tokens_ref.at[pl.ds(base, reach_rows), :], target, edge_sem.at[side]
        )
        receives = me > 0 if side == 0 else me < size - 1
        halos.append((there, receives, remote, edge))

        @pl.when(there)
        def _():
            remote.start()

        @pl.when(jnp.logical_not(receives))
        def _():
            edge.start()

    loads = [
        pltpu.make_async_copy(source, target, local_sem.at[i])
        for i, (source, target) in enumerate(
            ((tokens_ref, own), (wq_hbm, wq), (wk_hbm, wk), (wv_hbm, wv))
        )
    ]
    for load in loads:
        load.start()
    for load in loads:
        load.wait()

    def forward(k, c):
        j, targets = children(k)

        @pl.when(j > 0)
        def _():
            key_copy(k, c, 0, across, key_ref, k * frame_rows).wait_recv()
            for child, (there, device) in enumerate(targets):

                @pl.when(there)
                def _():
                    key_copy(k, c, child, device, key_ref, k * frame_rows).start()

    near_first = me < size // 2

    @pl.when(near_first)
    def _():
        for c in range(KEY_CHUNKS):
            forward(0, c)

    @pl.when(jnp.logical_not(near_first))
    def _():
        for c in range(KEY_CHUNKS):
            forward(1, c)

    step_rows = own_rows // PROJECTIONS
    every = KEY_CHUNKS // PROJECTIONS
    for c in range(KEY_CHUNKS):

        @pl.when(near_first)
        def _():
            forward(1, c)

        @pl.when(jnp.logical_not(near_first))
        def _():
            forward(0, c)

        if c % every != every - 1:
            continue
        at = pl.ds(c // every * step_rows, step_rows)
        rows = normalise(own[at, :], gain_ref[...])
        q = jnp.dot(rows, wq[...], preferred_element_type=jnp.float32)
        q_ref[at, :] = (q * (HEAD_DIM ** (-0.5) * math.log2(math.e))).astype(jnp.bfloat16)
        k_ref[at, :] = jnp.dot(rows, wk[...], preferred_element_type=jnp.float32).astype(jnp.bfloat16)
        v_ref[at, :] = jnp.dot(rows, wv[...], preferred_element_type=jnp.float32).astype(jnp.bfloat16)

    for there, receives, remote, edge in halos:

        @pl.when(receives)
        def _():
            remote.wait_recv()

        @pl.when(jnp.logical_not(receives))
        def _():
            edge.wait()

        @pl.when(there)
        def _():
            remote.wait_send()

    for k in range(2):
        j, targets = children(k)

        @pl.when(j == 0)
        def _():
            pltpu.make_async_copy(
                tokens_ref.at[pl.ds(0, frame_rows), :],
                key_ref.at[pl.ds(k * frame_rows, frame_rows), :],
                root_sem.at[k],
            ).wait()

        for c in range(KEY_CHUNKS):
            for child, (there, device) in enumerate(targets):

                @pl.when(there)
                def _():
                    key_copy(k, c, child, device, key_ref, k * frame_rows).wait_send()


def exchange(token_rows, gain, query_weight, key_weight, value_weight, size, frame_rows):
    own_rows, width = token_rows.shape
    shape = lambda rows: jax.ShapeDtypeStruct((rows, width), jnp.bfloat16)
    hbm = pl.BlockSpec(memory_space=pl.ANY)
    vmem = pl.BlockSpec(memory_space=pltpu.VMEM)
    reach_rows = FRAME_REACH * frame_rows
    dma = pltpu.SemaphoreType.DMA
    square = pltpu.VMEM((width, width), jnp.bfloat16)
    return pl.pallas_call(
        functools.partial(exchange_kernel, size, frame_rows),
        out_shape=(
            shape(reach_rows), shape(reach_rows), shape(2 * frame_rows),
            shape(own_rows), shape(own_rows), shape(own_rows),
        ),
        in_specs=[hbm, vmem, hbm, hbm, hbm],
        out_specs=(hbm, hbm, hbm, vmem, vmem, vmem),
        scratch_shapes=[
            pltpu.VMEM((own_rows, width), jnp.bfloat16), square, square, square,
            dma((2,)), dma((2,)), dma((2, KEY_CHUNKS, 3)), dma((2, KEY_CHUNKS)),
            dma((4,)), dma((2,)), dma((2,)),
        ],
        compiler_params=pltpu.CompilerParams(
            collective_id=0, has_side_effects=True, vmem_limit_bytes=40 * 2 ** 20
        ),
    )(token_rows, gain, query_weight, key_weight, value_weight)


def fused(tokens, norm_gain, query_weight, key_weight, value_weight, out_weight, key_frames):
    frame_count, band_count, band_tokens, width_model = tokens.shape
    frame_rows = band_count * band_tokens
    keyframe_count = key_frames.shape[0]
    size = lax.axis_size("tm")
    me = lax.axis_index("tm")
    frames_total = size * frame_count
    token_rows = tokens.reshape(-1, width_model)
    gain = norm_gain.reshape(1, -1)
    left, right, key_tokens, queries, key_rows, values = exchange(
        token_rows, gain, query_weight, key_weight, value_weight, size, frame_rows
    )
    first_frame = me * frame_count
    frame_now = first_frame + jnp.arange(frame_count, dtype=jnp.int32)
    window = frame_now[:, None] - FRAME_REACH + jnp.arange(2 * FRAME_REACH + 1, dtype=jnp.int32)[None]
    valid = jnp.concatenate(
        [
            (window >= 0) & (window < frames_total),
            jnp.abs(frame_now[:, None] - key_frames[None]) > FRAME_REACH,
        ],
        axis=1,
    )
    group = 512
    ext_rows = (2 * FRAME_REACH + frame_count + keyframe_count) * frame_rows
    own_rows = frame_count * frame_rows
    whole = lambda shape: pl.BlockSpec(shape, lambda i: (0, 0), pipeline_mode=pl.Buffered(1))
    columns = pl.BlockSpec((width_model, group), lambda i: (0, i))
    own_columns = pl.BlockSpec((own_rows, group), lambda i: (0, i))
    out = pl.pallas_call(
        functools.partial(fused_kernel, frame_count, band_count, band_tokens, keyframe_count),
        grid=(width_model // group,),
        out_shape=jax.ShapeDtypeStruct((own_rows, width_model), jnp.bfloat16),
        in_specs=[
            pl.BlockSpec(memory_space=pltpu.SMEM),
            whole((FRAME_REACH * frame_rows, width_model)),
            whole((own_rows, width_model)),
            whole((FRAME_REACH * frame_rows, width_model)),
            whole((keyframe_count * frame_rows, width_model)),
            whole((1, width_model)),
            own_columns, own_columns, own_columns,
            columns, columns,
            whole((width_model, width_model)),
        ],
        out_specs=whole((own_rows, width_model)),
        scratch_shapes=[
            pltpu.VMEM((ext_rows, width_model), jnp.bfloat16),
            pltpu.VMEM((ext_rows, group), jnp.bfloat16),
            pltpu.VMEM((ext_rows, group), jnp.bfloat16),
            pltpu.VMEM((own_rows, width_model), jnp.bfloat16),
        ],
        compiler_params=pltpu.CompilerParams(vmem_limit_bytes=56 * 2 ** 20),
    )(
        valid.astype(jnp.int32),
        left, token_rows, right, key_tokens, gain,
        queries, key_rows, values, key_weight, value_weight, out_weight,
    )
    return out.reshape(tokens.shape)


def solution(mesh):
    simple = mesh.shape["band"] == 1 and mesh.shape["tm"] % 4 == 0

    def body(*args):
        frames, keys = args[0].shape[0], args[6].shape[0]
        if simple and frames >= FRAME_REACH and keys == 2:
            return fused(*args)
        return per_device(*args)

    in_specs = (P(("slab", "tm"), "band", None, None), P(), P(), P(), P(), P(), P("slab"))
    out_specs = P(("slab", "tm"), "band", None, None)
    return jax.shard_map(
        body, mesh=mesh, in_specs=in_specs, out_specs=out_specs, check_vma=False
    )
```
